32 devices in a mesh: ctx: 4 (over y, x), head: 8 (over z, core).
Axes of the slice: x: 2, y: 2, z: 4, core: 2. Of those that a mesh axis runs over, the one named last changes fastest.
Arguments:
- queries: bfloat16 [32, 96, 4096], P(None, None, ('ctx', 'head')), may hold values from -9 to 9
- keys: bfloat16 [32, 96, 4096], P(None, None, ('ctx', 'head')), may hold values from -9 to 9
- values: bfloat16 [32, 96, 4096], P(None, None, ('ctx', 'head')), may hold values from -6 to 6
- doc_start: int32 [4096], P(('ctx', 'head')), may hold values from 0 to 4095, as said below
Outputs:
- grad_queries: bfloat16 [32, 96, 4096], P(None, None, ('ctx', 'head'))
- grad_keys: bfloat16 [32, 96, 4096], P(None, None, ('ctx', 'head'))
- grad_values: bfloat16 [32, 96, 4096], P(None, None, ('ctx', 'head'))
The draws below stay inside these ranges and needn't reach their ends.
Inputs may be any that keep to these rules, and one draw needn't show every extreme that they name: doc_start never falls; doc_start[t] is t or doc_start[t-1], t - doc_start[t] < 512, the first document has exactly 512 positions, and at every multiple k of 1024 after 0 a document starts at k - 256 and runs through k + 512 // 2 - 1.
All inputs are finite; a program needn't handle non-finite values.
Results may differ from the reference program's by a relative error of at most 0.02.
Values may be sent and summed in bfloat16 or wider, within the bound.
A program may use at most 128 MiB of HBM per device.

```python
import math
import jax
import jax.numpy as jnp
from jax import lax

HEADS = 32
HEAD_DIM = 96
TOK_DEV = 128
DOC_MAX = 512
TOKENS = 4096
N_HEAD = 8


def draw_queries(key, part):
    key = jax.random.fold_in(key, 3)
    planted = jnp.clip(jax.random.normal(key, (HEADS, HEAD_DIM, TOKENS)), -5.0, 5.0)
    return planted.astype(jnp.bfloat16)


def draw_keys(key, part):
    key = jax.random.fold_in(key, 5)
    planted = jnp.clip(jax.random.normal(key, (HEADS, HEAD_DIM, TOKENS)), -5.0, 5.0)
    return planted.astype(jnp.bfloat16)


def draw_doc_start(key, part):
    key = jax.random.fold_in(key, 7)
    rolls = jax.random.randint(key, (TOKENS,), 0, max(DOC_MAX // 4, 2))
    positions = jnp.arange(TOKENS, dtype=jnp.int32)
    group_span = TOK_DEV * N_HEAD
    half_doc = DOC_MAX // 2

    def advance(current, pair):
        position, roll = pair
        phase = position % group_span
        planted = (phase == group_span - half_doc) & (position >= DOC_MAX)
        banned = (phase > group_span - half_doc) | (phase < half_doc)
        chosen = (position >= DOC_MAX) & (roll == 0) & jnp.logical_not(banned)
        fresh = (position == 0) | planted | chosen | (position - current >= DOC_MAX)
        current = jnp.where(fresh, position, current)
        return (current, current)
    _, starts = lax.scan(advance, jnp.int32(0), (positions, rolls))
    return starts


def block_levels(own_key, dims, shards, smallest, top_value):
    gain, own = 1.0, jax.random.fold_in(own_key, 6)
    for dim, shards_of in shards:
        heights = jnp.exp(jax.random.uniform(jax.random.fold_in(own, dim), (shards_of,), jnp.float32, smallest / len(shards), top_value / len(shards)))
        gain = gain * jnp.repeat(heights, dims[dim] // shards_of).reshape([-1 if axis == dim else 1 for axis in range(len(dims))])
    return gain


def scatter_about(key, shape, deviation, reach, pieces=(), held_as=jnp.bfloat16):
    drawn = deviation * jax.random.normal(key, shape, jnp.float32)
    if pieces:
        drawn = drawn * block_levels(key, shape, pieces, -0.22, 0.18)
    return jnp.clip(drawn, -reach, reach).astype(held_as)


def setup_inputs(seed: int = 0) -> dict:
    arg_keys = jax.random.split(jax.random.key(seed), 5)
    return {
        "queries": draw_queries(jax.random.fold_in(arg_keys[4], 71), 0),
        "keys": draw_keys(jax.random.fold_in(arg_keys[4], 71), 0),
        "values": scatter_about(arg_keys[2], (HEADS, HEAD_DIM, TOKENS), 1.0, 6.0, ((2, 32),)),
        "doc_start": draw_doc_start(jax.random.fold_in(arg_keys[4], 71), 0),
    }


def block_grads(query_blk, key_win, value_win, first_pos, query_pos, key_pos, score_scale):
    visible = (key_pos[None, :] >= first_pos[:, None]) & (key_pos[None, :] <= query_pos[:, None])
    query_wide = query_blk.astype(jnp.float32)
    key_wide = key_win.astype(jnp.float32)
    value_wide = value_win.astype(jnp.float32)
    scores = jnp.einsum('hdq,hdk->hqk', query_wide, key_wide) * score_scale
    scores = jnp.where(visible[None], scores, -jnp.inf)
    row_peak = lax.optimization_barrier(jnp.max(scores, axis=2, keepdims=True))
    weights = jnp.exp(scores - row_peak)
    soft_probs = weights / lax.optimization_barrier(jnp.sum(weights, axis=2, keepdims=True))
    probs_low = lax.optimization_barrier(soft_probs.astype(jnp.bfloat16)).astype(jnp.float32)
    attended = jnp.einsum('hqk,hdk->hdq', probs_low, value_wide).astype(jnp.bfloat16)
    attended = lax.optimization_barrier(attended).astype(jnp.float32)
    grad_value = jnp.einsum('hqk,hdq->hdk', probs_low, attended)
    grad_probs = jnp.einsum('hdq,hdk->hqk', attended, value_wide)
    row_dot = lax.optimization_barrier(jnp.sum(attended * attended, axis=1))
    grad_scores = (soft_probs * (grad_probs - row_dot[:, :, None])).astype(jnp.bfloat16)
    grad_scores = lax.optimization_barrier(grad_scores).astype(jnp.float32)
    grad_query = (jnp.einsum('hqk,hdk->hdq', grad_scores, key_wide) * score_scale).astype(jnp.bfloat16)
    grad_key = jnp.einsum('hqk,hdq->hdk', grad_scores, query_wide)
    return (grad_query, grad_key, grad_value)

def reference(queries, keys, values, doc_start):
    head_count, head_depth, total = queries.shape
    score_scale = 1.0 / math.sqrt(head_depth)
    window = DOC_MAX
    blocks = total // window
    padding = jnp.zeros((head_count, head_depth, window), queries.dtype)
    key_ext = jnp.concatenate([padding, keys], axis=2)
    value_ext = jnp.concatenate([padding, values], axis=2)
    offsets = jnp.arange(window, dtype=jnp.int32)
    spread = jnp.arange(2 * window, dtype=jnp.int32)

    def one_block(near_prev, number):
        block_base = (number * window).astype(jnp.int32)
        query_blk = lax.dynamic_slice_in_dim(queries, block_base, window, 2)
        key_win = lax.dynamic_slice_in_dim(key_ext, block_base, 2 * window, 2)
        value_win = lax.dynamic_slice_in_dim(value_ext, block_base, 2 * window, 2)
        first_pos = lax.dynamic_slice_in_dim(doc_start, block_base, window, 0)
        query_pos = block_base + offsets
        key_pos = block_base - window + spread
        grad_query, grad_key, grad_value = block_grads(query_blk, key_win, value_win, first_pos, query_pos, key_pos, score_scale)
        done_key = ((near_prev[0] + grad_key[:, :, :window]) * score_scale).astype(jnp.bfloat16)
        done_value = (near_prev[1] + grad_value[:, :, :window]).astype(jnp.bfloat16)
        return ((grad_key[:, :, window:], grad_value[:, :, window:]), (grad_query, done_key, done_value))
    start_carry = (jnp.zeros((head_count, head_depth, window), jnp.float32), jnp.zeros((head_count, head_depth, window), jnp.float32))
    last_carry, (query_stack, key_stack, value_stack) = lax.scan(one_block, start_carry, jnp.arange(blocks, dtype=jnp.int32))
    last_key = (last_carry[0] * score_scale).astype(jnp.bfloat16)
    last_value = last_carry[1].astype(jnp.bfloat16)
    key_stack = jnp.concatenate([key_stack[1:], last_key[None]], axis=0)
    value_stack = jnp.concatenate([value_stack[1:], last_value[None]], axis=0)

    def to_whole(stacked):
        return jnp.moveaxis(stacked, 0, 2).reshape(head_count, head_depth, total)
    return (to_whole(query_stack), to_whole(key_stack), to_whole(value_stack))
```

```python
import functools
import math

import jax
import jax.numpy as jnp
from jax import lax
from jax.experimental import pallas as pl
from jax.experimental.pallas import tpu as pltpu
from jax.sharding import PartitionSpec as P

DOC_MAX = 512
PIECE = 2
MESH = pl.DeviceIdType.MESH


def from_behind(value, axis, steps):
    count = lax.axis_size(axis)
    first, last = (max(0, -steps), min(count, count - steps))
    return lax.ppermute(value, axis, [(source, source + steps) for source in range(first, last)])


def block_grads(query_blk, key_win, value_win, first_pos, query_pos, key_pos, score_scale):
    visible = (key_pos[None, :] >= first_pos[:, None]) & (key_pos[None, :] <= query_pos[:, None])
    scores = (
        jnp.einsum("hdq,hdk->hqk", query_blk, key_win, preferred_element_type=jnp.float32)
        * score_scale
    )
    scores = jnp.where(visible[None], scores, -jnp.inf)
    row_peak = jnp.max(scores, axis=2, keepdims=True)
    weights = jnp.exp(scores - row_peak)
    soft_probs = weights / jnp.sum(weights, axis=2, keepdims=True)
    probs_low = soft_probs.astype(jnp.bfloat16)
    attended = jnp.einsum(
        "hqk,hdk->hdq", probs_low, value_win, preferred_element_type=jnp.float32
    ).astype(jnp.bfloat16)
    grad_value = jnp.einsum("hqk,hdq->hdk", probs_low, attended, preferred_element_type=jnp.float32)
    grad_probs = jnp.einsum("hdq,hdk->hqk", attended, value_win, preferred_element_type=jnp.float32)
    wide_att = attended.astype(jnp.float32)
    row_dot = jnp.sum(wide_att * wide_att, axis=1)
    grad_scores = (soft_probs * (grad_probs - row_dot[:, :, None])).astype(jnp.bfloat16)
    grad_query = (
        jnp.einsum("hqk,hdk->hdq", grad_scores, key_win, preferred_element_type=jnp.float32)
        * score_scale
    ).astype(jnp.bfloat16)
    grad_key = jnp.einsum(
        "hqk,hdq->hdk", grad_scores, query_blk, preferred_element_type=jnp.float32
    )
    return (grad_query, grad_key, grad_value)


def shards(queries, keys, values, doc_start):
    score_scale = 1.0 / math.sqrt(queries.shape[1])
    head_q, head_k, head_v = (
        lax.all_to_all(queries, "head", split_axis=0, concat_axis=2, tiled=True),
        lax.all_to_all(keys, "head", split_axis=0, concat_axis=2, tiled=True),
        lax.all_to_all(values, "head", split_axis=0, concat_axis=2, tiled=True),
    )
    starts = lax.all_gather(doc_start, "head", axis=0, tiled=True)
    local_heads = head_q.shape[0]
    head_depth = head_q.shape[1]
    group_span = head_q.shape[2]
    window = DOC_MAX
    blocks = group_span // window
    prior_k, prior_v = from_behind(
        (head_k[:, :, group_span - window :], head_v[:, :, group_span - window :]), "ctx", 1
    )
    anchor = lax.axis_index("ctx") * group_span
    key_ext = jnp.concatenate([prior_k, head_k], axis=2).reshape(
        local_heads, head_depth, blocks + 1, window
    )
    value_ext = jnp.concatenate([prior_v, head_v], axis=2).reshape(
        local_heads, head_depth, blocks + 1, window
    )
    key_wins = jnp.moveaxis(jnp.concatenate([key_ext[:, :, :-1], key_ext[:, :, 1:]], axis=3), 2, 0)
    value_wins = jnp.moveaxis(
        jnp.concatenate([value_ext[:, :, :-1], value_ext[:, :, 1:]], axis=3), 2, 0
    )
    query_blocks = jnp.moveaxis(head_q.reshape(local_heads, head_depth, blocks, window), 2, 0)
    start_blocks = starts.reshape(blocks, window)
    offsets = jnp.arange(window, dtype=jnp.int32)
    spread = jnp.arange(2 * window, dtype=jnp.int32)

    def one_block(unused_carry, block_item):
        query_blk, key_win, value_win, first_pos, number = block_item
        block_base = anchor + number * window
        query_pos = block_base + offsets
        key_pos = block_base - window + spread
        return (
            unused_carry,
            block_grads(query_blk, key_win, value_win, first_pos, query_pos, key_pos, score_scale),
        )

    _, (query_stack, key_stack, value_stack) = lax.scan(
        one_block,
        jnp.int32(0),
        (query_blocks, key_wins, value_wins, start_blocks, jnp.arange(blocks, dtype=jnp.int32)),
    )
    far_k = key_stack[..., :window]
    far_v = value_stack[..., :window]
    own_k = key_stack[..., window:] + jnp.concatenate(
        [far_k[1:], jnp.zeros_like(far_k[:1])], axis=0
    )
    own_v = value_stack[..., window:] + jnp.concatenate(
        [far_v[1:], jnp.zeros_like(far_v[:1])], axis=0
    )
    back_k, back_v = from_behind((far_k[0], far_v[0]), "ctx", -1)
    own_k = own_k.at[blocks - 1].add(back_k)
    own_v = own_v.at[blocks - 1].add(back_v)

    def to_span(stacked):
        return jnp.moveaxis(stacked, 0, 2).reshape(local_heads, head_depth, group_span)

    grad_q = to_span(query_stack)
    grad_k = (to_span(own_k) * score_scale).astype(jnp.bfloat16)
    grad_v = to_span(own_v).astype(jnp.bfloat16)
    return (
        lax.all_to_all(grad_q, "head", split_axis=2, concat_axis=0, tiled=True),
        lax.all_to_all(grad_k, "head", split_axis=2, concat_axis=0, tiled=True),
        lax.all_to_all(grad_v, "head", split_axis=2, concat_axis=0, tiled=True),
    )


def chunk_kernel(
    n_ctx, n_head, q_ref, k_ref, v_ref, doc_ref, dq_ref, dk_ref, dv_ref,
    qbuf, kvbuf, dbuf, bias, stage_q, stage_kv, part,
    in_s, in_r, loc_in, doc_s, doc_r, l_s, l_r, g_s, g_r, o_s, o_r, loc_out,
):
    heads, depth, toks = q_ref.shape
    half = heads // 2
    pieces = half // PIECE
    scale = 1.0 / math.sqrt(depth)
    me = lax.axis_index("ctx") * n_head + lax.axis_index("head")
    chip, core = me // 2, me % 2
    mate = 1 - core
    last = n_ctx * n_head // 2 - 1
    odd = chip % 2
    is_left = (chip == 0) | ((odd == 1) & (chip >= 3) & (chip < last))
    is_right = (chip == 1) | ((odd == 0) & (chip >= 4))
    paired = is_left | is_right
    other_chip = jnp.where(is_left, chip + 1, chip - 1)

    def device(chip_id, core_id):
        linear = chip_id * 2 + core_id
        return (linear // n_head, linear % n_head)

    mate_id = device(chip, mate)

    def remote(src, dst, send, recv, to):
        return pltpu.make_async_remote_copy(
            src_ref=src, dst_ref=dst, send_sem=send, recv_sem=recv, device_id=to, device_id_type=MESH
        )

    def span(base, p):
        return pl.ds(base + p * PIECE, PIECE)

    def mate_in(i, p):
        src = (q_ref, k_ref, v_ref)[i].at[span(mate * half, p)]
        dst = qbuf.at[core, span(0, p)] if i == 0 else kvbuf.at[i - 1, 2 + core, span(0, p)]
        return remote(src, dst, in_s.at[i, p], in_r.at[i, p], mate_id)

    def own_in(i):
        src = (q_ref, k_ref, v_ref)[i].at[pl.ds(core * half, half)]
        dst = qbuf.at[core] if i == 0 else kvbuf.at[i - 1, 2 + core]
        return pltpu.make_async_copy(src, dst, loc_in.at[i])

    def doc_copy():
        return remote(doc_ref, dbuf.at[core], doc_s.at[0], doc_r.at[0], mate_id)

    def ahead(i, j, p):
        src = (k_ref, v_ref)[i].at[span(j * half, p)]
        return remote(
            src, kvbuf.at[i, core, span(0, p)], l_s.at[i, j, p], l_r.at[i, core, p], device(other_chip, j)
        )

    def ahead_arrival(i, j, p):
        src = (k_ref, v_ref)[i].at[span(j * half, p)]
        return remote(
            src, kvbuf.at[i, j, span(0, p)], l_s.at[i, j, p], l_r.at[i, j, p], device(other_chip, j)
        )

    def back(i, j, p):
        return remote(
            stage_kv.at[i, j, span(0, p)], part.at[i, core, span(0, p)],
            g_s.at[i, j, p], g_r.at[i, core, p], device(other_chip, j),
        )

    def back_arrival(i, j, p):
        return remote(
            stage_kv.at[i, j, span(0, p)], part.at[i, j, span(0, p)],
            g_s.at[i, j, p], g_r.at[i, j, p], device(other_chip, j),
        )

    def staged(i, whose, p):
        return stage_q.at[whose, span(0, p)] if i == 0 else stage_kv.at[i - 1, 2 + whose, span(0, p)]

    def mate_out(i, p):
        dst = (dq_ref, dk_ref, dv_ref)[i].at[span(core * half, p)]
        return remote(staged(i, mate, p), dst, o_s.at[i, p], o_r.at[i, p], mate_id)

    def mate_out_arrival(i, p):
        dst = (dq_ref, dk_ref, dv_ref)[i].at[span(mate * half, p)]
        return remote(staged(i, mate, p), dst, o_s.at[i, p], o_r.at[i, p], mate_id)

    def own_out(i, p):
        dst = (dq_ref, dk_ref, dv_ref)[i].at[span(core * half, p)]
        return pltpu.make_async_copy(staged(i, core, p), dst, loc_out.at[i, p])

    def each(body):
        lax.fori_loop(0, pieces, lambda p, carry: (body(p), carry)[1], 0)

    barrier = pltpu.get_barrier_semaphore()
    pl.semaphore_signal(barrier, inc=1, device_id=mate_id, device_id_type=MESH)

    @pl.when(paired)
    def _():
        for j in range(2):
            pl.semaphore_signal(barrier, inc=1, device_id=device(other_chip, j), device_id_type=MESH)
        pl.semaphore_wait(barrier, 3)

    @pl.when(jnp.logical_not(paired))
    def _():
        pl.semaphore_wait(barrier, 1)

    @pl.when(is_left)
    def _():
        def send(p):
            for j in range(2):
                for i in range(2):
                    ahead(i, j, p).start()

        each(send)

    doc_copy().start()
    for i in range(3):
        own_in(i).start()

    def send_mate(p):
        for i in range(3):
            mate_in(i, p).start()

    each(send_mate)
    dbuf[core] = doc_ref[...]
    for i in range(3):
        own_in(i).wait()
    doc_copy().wait_send()
    remote(doc_ref, dbuf.at[mate], doc_s.at[0], doc_r.at[0], mate_id).wait_recv()

    wide = 2 * toks
    base = chip * wide
    first = jnp.concatenate([dbuf[0], dbuf[1]], axis=1)
    query_pos = base + lax.broadcasted_iota(jnp.int32, (2 * wide, wide), 1)
    key_pos = base - wide + lax.broadcasted_iota(jnp.int32, (2 * wide, wide), 0)
    bias[...] = jnp.where((key_pos >= first) & (key_pos <= query_pos), 0.0, -jnp.inf)

    def one_head(h, slots):
        query = jnp.concatenate([qbuf[0, h], qbuf[1, h]], axis=1)
        key = jnp.concatenate([kvbuf[0, s, h] for s in slots], axis=1)
        value = jnp.concatenate([kvbuf[1, s, h] for s in slots], axis=1)
        rows = pl.ds(slots[0] * toks, len(slots) * toks)
        dot = functools.partial(lax.dot_general, preferred_element_type=jnp.float32)
        tn, nn, nt = ((((0,), (0,)), ((), ())), (((1,), (0,)), ((), ())), (((1,), (1,)), ((), ())))
        scores = dot(key, query, tn) * (scale * math.log2(math.e)) + bias[rows, :]
        weights = jnp.exp2(scores - jnp.max(scores, axis=0, keepdims=True))
        probs = weights * (1.0 / jnp.sum(weights, axis=0, keepdims=True))
        low = probs.astype(jnp.bfloat16)
        attended = dot(value, low, nn).astype(jnp.bfloat16)
        wide_att = attended.astype(jnp.float32)
        row_dot = jnp.sum(wide_att * wide_att, axis=0, keepdims=True)
        grad_probs = dot(value, attended, tn)
        grad_scores = (probs * (grad_probs - row_dot)).astype(jnp.bfloat16)
        grad_q = (dot(key, grad_scores, nn) * scale).astype(jnp.bfloat16)
        grad_k = (dot(query, grad_scores, nt) * scale).astype(jnp.bfloat16)
        grad_v = dot(attended, low, nt).astype(jnp.bfloat16)
        for j in range(2):
            stage_q[j, h] = grad_q[:, j * toks : (j + 1) * toks]
        for n, s in enumerate(slots):
            stage_kv[0, s, h] = grad_k[:, n * toks : (n + 1) * toks]
            stage_kv[1, s, h] = grad_v[:, n * toks : (n + 1) * toks]

    def work(p, slots):
        for i in range(3):
            dst = qbuf.at[mate, span(0, p)] if i == 0 else kvbuf.at[i - 1, 2 + mate, span(0, p)]
            src = (q_ref, k_ref, v_ref)[i].at[span(mate * half, p)]
            remote(src, dst, in_s.at[i, p], in_r.at[i, p], mate_id).wait_recv()
        for n in range(PIECE):
            one_head(p * PIECE + n, slots)
        for i in range(3):
            mate_out(i, p).start()
            own_out(i, p).start()

    @pl.when(is_right)
    def _():
        def step(p):
            for j in range(2):
                for i in range(2):
                    ahead_arrival(i, j, p).wait_recv()
            work(p, (0, 1, 2, 3))
            for j in range(2):
                for i in range(2):
                    back(i, j, p).start()

        each(step)

    @pl.when(jnp.logical_not(is_right))
    def _():
        each(lambda p: work(p, (2, 3)))

    def drain(p):
        for i in range(3):
            mate_in(i, p).wait_send()
            own_out(i, p).wait()
            mate_out(i, p).wait_send()
            mate_out_arrival(i, p).wait_recv()

    each(drain)

    @pl.when(is_left)
    def _():
        def add(p):
            for i in range(2):
                out = (dk_ref, dv_ref)[i]
                for j in range(2):
                    ahead(i, j, p).wait_send()
                    back_arrival(i, j, p).wait_recv()
                    at = span(j * half, p)
                    total = out[at].astype(jnp.float32) + part[i, j, span(0, p)].astype(jnp.float32)
                    out[at] = total.astype(jnp.bfloat16)

        each(add)

    @pl.when(is_right)
    def _():
        def sent(p):
            for j in range(2):
                for i in range(2):
                    back(i, j, p).wait_send()

        each(sent)


def chunk_shards(n_ctx, n_head, queries, keys, values, doc_start):
    heads, depth, toks = queries.shape
    half = heads // 2
    pieces = half // PIECE
    like = jax.ShapeDtypeStruct(queries.shape, jnp.bfloat16)
    vmem = pl.BlockSpec(memory_space=pltpu.VMEM)
    low, sem = jnp.bfloat16, pltpu.SemaphoreType.DMA
    return pl.pallas_call(
        functools.partial(chunk_kernel, n_ctx, n_head),
        out_shape=(like, like, like),
        in_specs=[vmem] * 4,
        out_specs=(vmem,) * 3,
        scratch_shapes=[
            pltpu.VMEM((2, half, depth, toks), low),
            pltpu.VMEM((2, 4, half, depth, toks), low),
            pltpu.VMEM((2, 1, toks), jnp.int32),
            pltpu.VMEM((4 * toks, 2 * toks), jnp.float32),
            pltpu.VMEM((2, half, depth, toks), low),
            pltpu.VMEM((2, 4, half, depth, toks), low),
            pltpu.VMEM((2, 2, half, depth, toks), low),
            sem((3, pieces)), sem((3, pieces)), sem((3,)), sem((1,)), sem((1,)),
            sem((2, 2, pieces)), sem((2, 2, pieces)), sem((2, 2, pieces)), sem((2, 2, pieces)),
            sem((3, pieces)), sem((3, pieces)), sem((3, pieces)),
        ],
        compiler_params=pltpu.CompilerParams(
            collective_id=0, has_side_effects=True, vmem_limit_bytes=40 * 1024 * 1024
        ),
        cost_estimate=pl.CostEstimate(
            flops=12 * half * 8 * toks * toks * depth, bytes_accessed=12 * heads * depth * toks,
            transcendentals=8 * half * toks * toks,
        ),
    )(queries, keys, values, doc_start.reshape(1, toks))


def solution(mesh):
    n_ctx, n_head = mesh.shape["ctx"], mesh.shape["head"]

    def program(queries, keys, values, doc_start):
        toks = queries.shape[2]
        if 4 * toks == DOC_MAX and n_head * toks == 2 * DOC_MAX and queries.shape[0] % (2 * PIECE) == 0:
            return chunk_shards(n_ctx, n_head, queries, keys, values, doc_start)
        return shards(queries, keys, values, doc_start)

    spec = P(None, None, ("ctx", "head"))
    return jax.shard_map(
        program,
        mesh=mesh,
        in_specs=(spec, spec, spec, P(("ctx", "head"))),
        out_specs=(spec, spec, spec),
        check_vma=False,
    )
```

```python
import functools
import math

import jax
import jax.numpy as jnp
from jax import lax
from jax.experimental import pallas as pl
from jax.experimental.pallas import tpu as pltpu
from jax.sharding import PartitionSpec as P

DOC_MAX = 512
PIECE = 2
MESH = pl.DeviceIdType.MESH


def from_behind(value, axis, steps):
    count = lax.axis_size(axis)
    first, last = (max(0, -steps), min(count, count - steps))
    return lax.ppermute(value, axis, [(source, source + steps) for source in range(first, last)])


def block_grads(query_blk, key_win, value_win, first_pos, query_pos, key_pos, score_scale):
    visible = (key_pos[None, :] >= first_pos[:, None]) & (key_pos[None, :] <= query_pos[:, None])
    scores = (
        jnp.einsum("hdq,hdk->hqk", query_blk, key_win, preferred_element_type=jnp.float32)
        * score_scale
    )
    scores = jnp.where(visible[None], scores, -jnp.inf)
    row_peak = jnp.max(scores, axis=2, keepdims=True)
    weights = jnp.exp(scores - row_peak)
    soft_probs = weights / jnp.sum(weights, axis=2, keepdims=True)
    probs_low = soft_probs.astype(jnp.bfloat16)
    attended = jnp.einsum(
        "hqk,hdk->hdq", probs_low, value_win, preferred_element_type=jnp.float32
    ).astype(jnp.bfloat16)
    grad_value = jnp.einsum("hqk,hdq->hdk", probs_low, attended, preferred_element_type=jnp.float32)
    grad_probs = jnp.einsum("hdq,hdk->hqk", attended, value_win, preferred_element_type=jnp.float32)
    wide_att = attended.astype(jnp.float32)
    row_dot = jnp.sum(wide_att * wide_att, axis=1)
    grad_scores = (soft_probs * (grad_probs - row_dot[:, :, None])).astype(jnp.bfloat16)
    grad_query = (
        jnp.einsum("hqk,hdk->hdq", grad_scores, key_win, preferred_element_type=jnp.float32)
        * score_scale
    ).astype(jnp.bfloat16)
    grad_key = jnp.einsum(
        "hqk,hdq->hdk", grad_scores, query_blk, preferred_element_type=jnp.float32
    )
    return (grad_query, grad_key, grad_value)


def shards(queries, keys, values, doc_start):
    score_scale = 1.0 / math.sqrt(queries.shape[1])
    head_q, head_k, head_v = (
        lax.all_to_all(queries, "head", split_axis=0, concat_axis=2, tiled=True),
        lax.all_to_all(keys, "head", split_axis=0, concat_axis=2, tiled=True),
        lax.all_to_all(values, "head", split_axis=0, concat_axis=2, tiled=True),
    )
    starts = lax.all_gather(doc_start, "head", axis=0, tiled=True)
    local_heads = head_q.shape[0]
    head_depth = head_q.shape[1]
    group_span = head_q.shape[2]
    window = DOC_MAX
    blocks = group_span // window
    prior_k, prior_v = from_behind(
        (head_k[:, :, group_span - window :], head_v[:, :, group_span - window :]), "ctx", 1
    )
    anchor = lax.axis_index("ctx") * group_span
    key_ext = jnp.concatenate([prior_k, head_k], axis=2).reshape(
        local_heads, head_depth, blocks + 1, window
    )
    value_ext = jnp.concatenate([prior_v, head_v], axis=2).reshape(
        local_heads, head_depth, blocks + 1, window
    )
    key_wins = jnp.moveaxis(jnp.concatenate([key_ext[:, :, :-1], key_ext[:, :, 1:]], axis=3), 2, 0)
    value_wins = jnp.moveaxis(
        jnp.concatenate([value_ext[:, :, :-1], value_ext[:, :, 1:]], axis=3), 2, 0
    )
    query_blocks = jnp.moveaxis(head_q.reshape(local_heads, head_depth, blocks, window), 2, 0)
    start_blocks = starts.reshape(blocks, window)
    offsets = jnp.arange(window, dtype=jnp.int32)
    spread = jnp.arange(2 * window, dtype=jnp.int32)

    def one_block(unused_carry, block_item):
        query_blk, key_win, value_win, first_pos, number = block_item
        block_base = anchor + number * window
        query_pos = block_base + offsets
        key_pos = block_base - window + spread
        return (
            unused_carry,
            block_grads(query_blk, key_win, value_win, first_pos, query_pos, key_pos, score_scale),
        )

    _, (query_stack, key_stack, value_stack) = lax.scan(
        one_block,
        jnp.int32(0),
        (query_blocks, key_wins, value_wins, start_blocks, jnp.arange(blocks, dtype=jnp.int32)),
    )
    far_k = key_stack[..., :window]
    far_v = value_stack[..., :window]
    own_k = key_stack[..., window:] + jnp.concatenate(
        [far_k[1:], jnp.zeros_like(far_k[:1])], axis=0
    )
    own_v = value_stack[..., window:] + jnp.concatenate(
        [far_v[1:], jnp.zeros_like(far_v[:1])], axis=0
    )
    back_k, back_v = from_behind((far_k[0], far_v[0]), "ctx", -1)
    own_k = own_k.at[blocks - 1].add(back_k)
    own_v = own_v.at[blocks - 1].add(back_v)

    def to_span(stacked):
        return jnp.moveaxis(stacked, 0, 2).reshape(local_heads, head_depth, group_span)

    grad_q = to_span(query_stack)
    grad_k = (to_span(own_k) * score_scale).astype(jnp.bfloat16)
    grad_v = to_span(own_v).astype(jnp.bfloat16)
    return (
        lax.all_to_all(grad_q, "head", split_axis=2, concat_axis=0, tiled=True),
        lax.all_to_all(grad_k, "head", split_axis=2, concat_axis=0, tiled=True),
        lax.all_to_all(grad_v, "head", split_axis=2, concat_axis=0, tiled=True),
    )


def chunk_kernel(
    n_ctx, n_head, q_ref, k_ref, v_ref, doc_ref, dq_ref, dk_ref, dv_ref,
    qbuf, kvbuf, dbuf, bias, stage_q, stage_kv, part,
    in_s, in_r, loc_in, doc_s, doc_r, l_s, l_r, g_s, g_r, o_s, o_r, loc_out,
):
    heads, depth, toks = q_ref.shape
    half = heads // 2
    pieces = half // PIECE
    scale = 1.0 / math.sqrt(depth)
    me = lax.axis_index("ctx") * n_head + lax.axis_index("head")
    chip, core = me // 2, me % 2
    mate = 1 - core
    last = n_ctx * n_head // 2 - 1
    odd = chip % 2
    is_left = (chip == 0) | ((odd == 1) & (chip >= 3) & (chip < last))
    is_right = (chip == 1) | ((odd == 0) & (chip >= 4))
    paired = is_left | is_right
    other_chip = jnp.where(is_left, chip + 1, chip - 1)

    def device(chip_id, core_id):
        linear = chip_id * 2 + core_id
        return (linear // n_head, linear % n_head)

    mate_id = device(chip, mate)

    def remote(src, dst, send, recv, to):
        return pltpu.make_async_remote_copy(
            src_ref=src, dst_ref=dst, send_sem=send, recv_sem=recv, device_id=to, device_id_type=MESH
        )

    def span(base, p):
        return pl.ds(base + p * PIECE, PIECE)

    def mate_in(i, p):
        src = (q_ref, k_ref, v_ref)[i].at[span(mate * half, p)]
        dst = qbuf.at[core, span(0, p)] if i == 0 else kvbuf.at[i - 1, 2 + core, span(0, p)]
        return remote(src, dst, in_s.at[i, p], in_r.at[i, p], mate_id)

    def own_in(i):
        src = (q_ref, k_ref, v_ref)[i].at[pl.ds(core * half, half)]
        dst = qbuf.at[core] if i == 0 else kvbuf.at[i - 1, 2 + core]
        return pltpu.make_async_copy(src, dst, loc_in.at[i])

    def doc_copy():
        return remote(doc_ref, dbuf.at[core], doc_s.at[0], doc_r.at[0], mate_id)

    def ahead(i, j, p):
        src = (k_ref, v_ref)[i].at[span(j * half, p)]
        return remote(
            src, kvbuf.at[i, core, span(0, p)], l_s.at[i, j, p], l_r.at[i, core, p], device(other_chip, j)
        )

    def ahead_arrival(i, j, p):
        src = (k_ref, v_ref)[i].at[span(j * half, p)]
        return remote(
            src, kvbuf.at[i, j, span(0, p)], l_s.at[i, j, p], l_r.at[i, j, p], device(other_chip, j)
        )

    def back(i, j, p):
        return remote(
            stage_kv.at[i, j, span(0, p)], part.at[i, core, span(0, p)],
            g_s.at[i, j, p], g_r.at[i, core, p], device(other_chip, j),
        )

    def back_arrival(i, j, p):
        return remote(
            stage_kv.at[i, j, span(0, p)], part.at[i, j, span(0, p)],
            g_s.at[i, j, p], g_r.at[i, j, p], device(other_chip, j),
        )

    def staged(i, whose, p):
        return stage_q.at[whose, span(0, p)] if i == 0 else stage_kv.at[i - 1, 2 + whose, span(0, p)]

    def mate_out(i, p):
        dst = (dq_ref, dk_ref, dv_ref)[i].at[span(core * half, p)]
        return remote(staged(i, mate, p), dst, o_s.at[i, p], o_r.at[i, p], mate_id)

    def mate_out_arrival(i, p):
        dst = (dq_ref, dk_ref, dv_ref)[i].at[span(mate * half, p)]
        return remote(staged(i, mate, p), dst, o_s.at[i, p], o_r.at[i, p], mate_id)

    def own_out(i, p):
        dst = (dq_ref, dk_ref, dv_ref)[i].at[span(core * half, p)]
        return pltpu.make_async_copy(staged(i, core, p), dst, loc_out.at[i, p])

    def each(body):
        lax.fori_loop(0, pieces, lambda p, carry: (body(p), carry)[1], 0)

    barrier = pltpu.get_barrier_semaphore()
    pl.semaphore_signal(barrier, inc=1, device_id=mate_id, device_id_type=MESH)

    @pl.when(paired)
    def _():
        for j in range(2):
            pl.semaphore_signal(barrier, inc=1, device_id=device(other_chip, j), device_id_type=MESH)
        pl.semaphore_wait(barrier, 3)

    @pl.when(jnp.logical_not(paired))
    def _():
        pl.semaphore_wait(barrier, 1)

    @pl.when(is_left)
    def _():
        def send(p):
            for j in range(2):
                for i in range(2):
                    ahead(i, j, p).start()

        each(send)

    doc_copy().start()
    for i in range(3):
        own_in(i).start()

    def send_mate(p):
        for i in range(3):
            mate_in(i, p).start()

    each(send_mate)
    dbuf[core] = doc_ref[...]
    for i in range(3):
        own_in(i).wait()
    doc_copy().wait_send()
    remote(doc_ref, dbuf.at[mate], doc_s.at[0], doc_r.at[0], mate_id).wait_recv()

    wide = 2 * toks
    base = chip * wide
    first = jnp.concatenate([dbuf[0], dbuf[1]], axis=1)
    query_pos = base + lax.broadcasted_iota(jnp.int32, (2 * wide, wide), 1)
    key_pos = base - wide + lax.broadcasted_iota(jnp.int32, (2 * wide, wide), 0)
    bias[...] = jnp.where((key_pos >= first) & (key_pos <= query_pos), 0.0, -jnp.inf)

    def one_head(h, slots):
        query = jnp.concatenate([qbuf[0, h], qbuf[1, h]], axis=1)
        key = jnp.concatenate([kvbuf[0, s, h] for s in slots], axis=1)
        value = jnp.concatenate([kvbuf[1, s, h] for s in slots], axis=1)
        rows = pl.ds(slots[0] * toks, len(slots) * toks)
        dot = functools.partial(lax.dot_general, preferred_element_type=jnp.float32)
        tn, nn, nt = ((((0,), (0,)), ((), ())), (((1,), (0,)), ((), ())), (((1,), (1,)), ((), ())))
        scores = dot(key, query, tn) * (scale * math.log2(math.e)) + bias[rows, :]
        weights = jnp.exp2(scores - jnp.max(scores, axis=0, keepdims=True))
        probs = weights * (1.0 / jnp.sum(weights, axis=0, keepdims=True))
        low = probs.astype(jnp.bfloat16)
        attended = dot(value, low, nn).astype(jnp.bfloat16)
        wide_att = attended.astype(jnp.float32)
        row_dot = jnp.sum(wide_att * wide_att, axis=0, keepdims=True)
        grad_probs = dot(value, attended, tn)
        grad_scores = (probs * (grad_probs - row_dot)).astype(jnp.bfloat16)
        grad_q = (dot(key, grad_scores, nn) * scale).astype(jnp.bfloat16)
        grad_k = (dot(query, grad_scores, nt) * scale).astype(jnp.bfloat16)
        grad_v = dot(attended, low, nt).astype(jnp.bfloat16)
        for j in range(2):
            stage_q[j, h] = grad_q[:, j * toks : (j + 1) * toks]
        for n, s in enumerate(slots):
            stage_kv[0, s, h] = grad_k[:, n * toks : (n + 1) * toks]
            stage_kv[1, s, h] = grad_v[:, n * toks : (n + 1) * toks]

    def work(p, slots):
        for i in range(3):
            dst = qbuf.at[mate, span(0, p)] if i == 0 else kvbuf.at[i - 1, 2 + mate, span(0, p)]
            src = (q_ref, k_ref, v_ref)[i].at[span(mate * half, p)]
            remote(src, dst, in_s.at[i, p], in_r.at[i, p], mate_id).wait_recv()
        for n in range(PIECE):
            one_head(p * PIECE + n, slots)
        for i in range(3):
            mate_out(i, p).start()
            own_out(i, p).start()

    @pl.when(is_right)
    def _():
        def send_back(p):
            for j in range(2):
                for i in range(2):
                    back(i, j, p).start()

        def step(p):
            for j in range(2):
                for i in range(2):
                    ahead_arrival(i, j, p).wait_recv()

            @pl.when(p == pieces - 1)
            def _():
                lax.fori_loop(0, pieces - 1, lambda e, carry: (send_back(e), carry)[1], 0)

            work(p, (0, 1, 2, 3))

        each(step)
        send_back(pieces - 1)

    @pl.when(jnp.logical_not(is_right))
    def _():
        each(lambda p: work(p, (2, 3)))

    def drain(p):
        for i in range(3):
            mate_in(i, p).wait_send()
            own_out(i, p).wait()
            mate_out(i, p).wait_send()
            mate_out_arrival(i, p).wait_recv()

    each(drain)

    @pl.when(is_left)
    def _():
        def add(p):
            for i in range(2):
                out = (dk_ref, dv_ref)[i]
                for j in range(2):
                    ahead(i, j, p).wait_send()
                    back_arrival(i, j, p).wait_recv()
                    at = span(j * half, p)
                    total = out[at].astype(jnp.float32) + part[i, j, span(0, p)].astype(jnp.float32)
                    out[at] = total.astype(jnp.bfloat16)

        each(add)

    @pl.when(is_right)
    def _():
        def sent(p):
            for j in range(2):
                for i in range(2):
                    back(i, j, p).wait_send()

        each(sent)


def chunk_shards(n_ctx, n_head, queries, keys, values, doc_start):
    heads, depth, toks = queries.shape
    half = heads // 2
    pieces = half // PIECE
    like = jax.ShapeDtypeStruct(queries.shape, jnp.bfloat16)
    vmem = pl.BlockSpec(memory_space=pltpu.VMEM)
    low, sem = jnp.bfloat16, pltpu.SemaphoreType.DMA
    return pl.pallas_call(
        functools.partial(chunk_kernel, n_ctx, n_head),
        out_shape=(like, like, like),
        in_specs=[pl.BlockSpec(memory_space=pltpu.HBM)] * 3 + [vmem],
        out_specs=(vmem,) * 3,
        scratch_shapes=[
            pltpu.VMEM((2, half, depth, toks), low),
            pltpu.VMEM((2, 4, half, depth, toks), low),
            pltpu.VMEM((2, 1, toks), jnp.int32),
            pltpu.VMEM((4 * toks, 2 * toks), jnp.float32),
            pltpu.VMEM((2, half, depth, toks), low),
            pltpu.VMEM((2, 4, half, depth, toks), low),
            pltpu.VMEM((2, 2, half, depth, toks), low),
            sem((3, pieces)), sem((3, pieces)), sem((3,)), sem((1,)), sem((1,)),
            sem((2, 2, pieces)), sem((2, 2, pieces)), sem((2, 2, pieces)), sem((2, 2, pieces)),
            sem((3, pieces)), sem((3, pieces)), sem((3, pieces)),
        ],
        compiler_params=pltpu.CompilerParams(
            collective_id=0, has_side_effects=True, vmem_limit_bytes=60 * 1024 * 1024
        ),
        cost_estimate=pl.CostEstimate(
            flops=12 * half * 8 * toks * toks * depth, bytes_accessed=12 * heads * depth * toks,
            transcendentals=8 * half * toks * toks,
        ),
    )(queries, keys, values, doc_start.reshape(1, toks))


def solution(mesh):
    n_ctx, n_head = mesh.shape["ctx"], mesh.shape["head"]

    def program(queries, keys, values, doc_start):
        toks = queries.shape[2]
        if 4 * toks == DOC_MAX and n_head * toks == 2 * DOC_MAX and queries.shape[0] % (2 * PIECE) == 0:
            return chunk_shards(n_ctx, n_head, queries, keys, values, doc_start)
        return shards(queries, keys, values, doc_start)

    spec = P(None, None, ("ctx", "head"))
    return jax.shard_map(
        program,
        mesh=mesh,
        in_specs=(spec, spec, spec, P(("ctx", "head"))),
        out_specs=(spec, spec, spec),
        check_vma=False,
    )
```

```python
import functools
import math

import jax
import jax.numpy as jnp
from jax import lax
from jax.experimental import pallas as pl
from jax.experimental.pallas import tpu as pltpu
from jax.sharding import PartitionSpec as P

DOC_MAX = 512
PIECE = 2
DETOUR = 2
MESH = pl.DeviceIdType.MESH


def from_behind(value, axis, steps):
    count = lax.axis_size(axis)
    first, last = (max(0, -steps), min(count, count - steps))
    return lax.ppermute(value, axis, [(source, source + steps) for source in range(first, last)])


def block_grads(query_blk, key_win, value_win, first_pos, query_pos, key_pos, score_scale):
    visible = (key_pos[None, :] >= first_pos[:, None]) & (key_pos[None, :] <= query_pos[:, None])
    scores = (
        jnp.einsum("hdq,hdk->hqk", query_blk, key_win, preferred_element_type=jnp.float32)
        * score_scale
    )
    scores = jnp.where(visible[None], scores, -jnp.inf)
    row_peak = jnp.max(scores, axis=2, keepdims=True)
    weights = jnp.exp(scores - row_peak)
    soft_probs = weights / jnp.sum(weights, axis=2, keepdims=True)
    probs_low = soft_probs.astype(jnp.bfloat16)
    attended = jnp.einsum(
        "hqk,hdk->hdq", probs_low, value_win, preferred_element_type=jnp.float32
    ).astype(jnp.bfloat16)
    grad_value = jnp.einsum("hqk,hdq->hdk", probs_low, attended, preferred_element_type=jnp.float32)
    grad_probs = jnp.einsum("hdq,hdk->hqk", attended, value_win, preferred_element_type=jnp.float32)
    wide_att = attended.astype(jnp.float32)
    row_dot = jnp.sum(wide_att * wide_att, axis=1)
    grad_scores = (soft_probs * (grad_probs - row_dot[:, :, None])).astype(jnp.bfloat16)
    grad_query = (
        jnp.einsum("hqk,hdk->hdq", grad_scores, key_win, preferred_element_type=jnp.float32)
        * score_scale
    ).astype(jnp.bfloat16)
    grad_key = jnp.einsum(
        "hqk,hdq->hdk", grad_scores, query_blk, preferred_element_type=jnp.float32
    )
    return (grad_query, grad_key, grad_value)


def shards(queries, keys, values, doc_start):
    score_scale = 1.0 / math.sqrt(queries.shape[1])
    head_q, head_k, head_v = (
        lax.all_to_all(queries, "head", split_axis=0, concat_axis=2, tiled=True),
        lax.all_to_all(keys, "head", split_axis=0, concat_axis=2, tiled=True),
        lax.all_to_all(values, "head", split_axis=0, concat_axis=2, tiled=True),
    )
    starts = lax.all_gather(doc_start, "head", axis=0, tiled=True)
    local_heads = head_q.shape[0]
    head_depth = head_q.shape[1]
    group_span = head_q.shape[2]
    window = DOC_MAX
    blocks = group_span // window
    prior_k, prior_v = from_behind(
        (head_k[:, :, group_span - window :], head_v[:, :, group_span - window :]), "ctx", 1
    )
    anchor = lax.axis_index("ctx") * group_span
    key_ext = jnp.concatenate([prior_k, head_k], axis=2).reshape(
        local_heads, head_depth, blocks + 1, window
    )
    value_ext = jnp.concatenate([prior_v, head_v], axis=2).reshape(
        local_heads, head_depth, blocks + 1, window
    )
    key_wins = jnp.moveaxis(jnp.concatenate([key_ext[:, :, :-1], key_ext[:, :, 1:]], axis=3), 2, 0)
    value_wins = jnp.moveaxis(
        jnp.concatenate([value_ext[:, :, :-1], value_ext[:, :, 1:]], axis=3), 2, 0
    )
    query_blocks = jnp.moveaxis(head_q.reshape(local_heads, head_depth, blocks, window), 2, 0)
    start_blocks = starts.reshape(blocks, window)
    offsets = jnp.arange(window, dtype=jnp.int32)
    spread = jnp.arange(2 * window, dtype=jnp.int32)

    def one_block(unused_carry, block_item):
        query_blk, key_win, value_win, first_pos, number = block_item
        block_base = anchor + number * window
        query_pos = block_base + offsets
        key_pos = block_base - window + spread
        return (
            unused_carry,
            block_grads(query_blk, key_win, value_win, first_pos, query_pos, key_pos, score_scale),
        )

    _, (query_stack, key_stack, value_stack) = lax.scan(
        one_block,
        jnp.int32(0),
        (query_blocks, key_wins, value_wins, start_blocks, jnp.arange(blocks, dtype=jnp.int32)),
    )
    far_k = key_stack[..., :window]
    far_v = value_stack[..., :window]
    own_k = key_stack[..., window:] + jnp.concatenate(
        [far_k[1:], jnp.zeros_like(far_k[:1])], axis=0
    )
    own_v = value_stack[..., window:] + jnp.concatenate(
        [far_v[1:], jnp.zeros_like(far_v[:1])], axis=0
    )
    back_k, back_v = from_behind((far_k[0], far_v[0]), "ctx", -1)
    own_k = own_k.at[blocks - 1].add(back_k)
    own_v = own_v.at[blocks - 1].add(back_v)

    def to_span(stacked):
        return jnp.moveaxis(stacked, 0, 2).reshape(local_heads, head_depth, group_span)

    grad_q = to_span(query_stack)
    grad_k = (to_span(own_k) * score_scale).astype(jnp.bfloat16)
    grad_v = to_span(own_v).astype(jnp.bfloat16)
    return (
        lax.all_to_all(grad_q, "head", split_axis=2, concat_axis=0, tiled=True),
        lax.all_to_all(grad_k, "head", split_axis=2, concat_axis=0, tiled=True),
        lax.all_to_all(grad_v, "head", split_axis=2, concat_axis=0, tiled=True),
    )


def chunk_kernel(
    n_ctx, n_head, q_ref, k_ref, v_ref, doc_ref, dq_ref, dk_ref, dv_ref,
    qbuf, kvbuf, dbuf, bias, stage_q, stage_kv, part,
    in_s, in_r, loc_in, doc_s, doc_r, l_s, l_r, g_s, g_r, o_s, o_r, loc_out, rbuf, r_s, r_r,
):
    heads, depth, toks = q_ref.shape
    half = heads // 2
    pieces = half // PIECE
    scale = 1.0 / math.sqrt(depth)
    me = lax.axis_index("ctx") * n_head + lax.axis_index("head")
    chip, core = me // 2, me % 2
    mate = 1 - core
    last = n_ctx * n_head // 2 - 1
    odd = chip % 2
    is_left = (chip == 0) | ((odd == 1) & (chip >= 3) & (chip < last))
    is_right = (chip == 1) | ((odd == 0) & (chip >= 4))
    paired = is_left | is_right
    other_chip = jnp.where(is_left, chip + 1, chip - 1)

    flows = n_ctx - 1
    items = flows * DETOUR
    chained = paired & (chip >= 3)
    flow = (chip + 1) // 4 - 1
    far = (chip + 1) % 4 < 2
    ahead_relay, back_relay = jnp.where(far, last, 1), jnp.where(far, 0, 2)
    relays_ahead = (chip == last) | (chip == 1)
    relays_back = (chip == 0) | (chip == 2)
    relays = relays_ahead | relays_back
    far_relay = (chip == last) | (chip == 0)

    def relay_ends(f):
        left = 4 * f + 4 + jnp.where(far_relay, -1, 1)
        return jnp.where(relays_ahead, left, left + 1), jnp.where(relays_ahead, left + 1, left)

    def device(chip_id, core_id):
        linear = chip_id * 2 + core_id
        return (linear // n_head, linear % n_head)

    mate_id = device(chip, mate)

    def remote(src, dst, send, recv, to):
        return pltpu.make_async_remote_copy(
            src_ref=src, dst_ref=dst, send_sem=send, recv_sem=recv, device_id=to, device_id_type=MESH
        )

    def span(base, p):
        return pl.ds(base + p * PIECE, PIECE)

    def mate_in(i, p):
        src = (q_ref, k_ref, v_ref)[i].at[span(mate * half, p)]
        dst = qbuf.at[core, span(0, p)] if i == 0 else kvbuf.at[i - 1, 2 + core, span(0, p)]
        return remote(src, dst, in_s.at[i, p], in_r.at[i, p], mate_id)

    def own_in(i):
        src = (q_ref, k_ref, v_ref)[i].at[pl.ds(core * half, half)]
        dst = qbuf.at[core] if i == 0 else kvbuf.at[i - 1, 2 + core]
        return pltpu.make_async_copy(src, dst, loc_in.at[i])

    def doc_copy():
        return remote(doc_ref, dbuf.at[core], doc_s.at[0], doc_r.at[0], mate_id)

    def ahead(i, j, p):
        src = (k_ref, v_ref)[i].at[span(j * half, p)]
        return remote(
            src, kvbuf.at[i, core, span(0, p)], l_s.at[i, j, p], l_r.at[i, core, p], device(other_chip, j)
        )

    def ahead_arrival(i, j, p):
        src = (k_ref, v_ref)[i].at[span(j * half, p)]
        return remote(
            src, kvbuf.at[i, j, span(0, p)], l_s.at[i, j, p], l_r.at[i, j, p], device(other_chip, j)
        )

    def back(i, j, p):
        return remote(
            stage_kv.at[i, j, span(0, p)], part.at[i, core, span(0, p)],
            g_s.at[i, j, p], g_r.at[i, core, p], device(other_chip, j),
        )

    def back_arrival(i, j, p):
        return remote(
            stage_kv.at[i, j, span(0, p)], part.at[i, j, span(0, p)],
            g_s.at[i, j, p], g_r.at[i, j, p], device(other_chip, j),
        )

    def ahead_detour(i, j, r):
        p = pieces - DETOUR + r
        src = (k_ref, v_ref)[i].at[span(j * half, p)]
        return remote(
            src, rbuf.at[flow, i, j, r], l_s.at[i, j, p], r_r.at[flow, i, j, r], device(ahead_relay, core)
        )

    def back_detour(i, j, r):
        return remote(
            stage_kv.at[i, j, span(0, r)], rbuf.at[flow, i, j, r],
            g_s.at[i, j, r], r_r.at[flow, i, j, r], device(back_relay, core),
        )

    def detour_arrival(f, i, j, r):
        return remote(
            rbuf.at[f, i, j, r], rbuf.at[f, i, j, r], r_s.at[f, i, j, r], r_r.at[f, i, j, r],
            device(relay_ends(f)[1], j),
        )

    def ahead_onward(f, i, j, r):
        p = pieces - DETOUR + r
        return remote(
            rbuf.at[f, i, j, r], kvbuf.at[i, core, span(0, p)],
            r_s.at[f, i, j, r], l_r.at[i, core, p], device(relay_ends(f)[1], j),
        )

    def back_onward(f, i, j, r):
        return remote(
            rbuf.at[f, i, j, r], part.at[i, core, span(0, r)],
            r_s.at[f, i, j, r], g_r.at[i, core, r], device(relay_ends(f)[1], j),
        )

    def relay(onward, item):
        f, r = item % flows, item // flows
        for j in range(2):
            for i in range(2):
                detour_arrival(f, i, j, r).wait_recv()
                onward(f, i, j, r).start()

    def staged(i, whose, p):
        return stage_q.at[whose, span(0, p)] if i == 0 else stage_kv.at[i - 1, 2 + whose, span(0, p)]

    def mate_out(i, p):
        dst = (dq_ref, dk_ref, dv_ref)[i].at[span(core * half, p)]
        return remote(staged(i, mate, p), dst, o_s.at[i, p], o_r.at[i, p], mate_id)

    def mate_out_arrival(i, p):
        dst = (dq_ref, dk_ref, dv_ref)[i].at[span(mate * half, p)]
        return remote(staged(i, mate, p), dst, o_s.at[i, p], o_r.at[i, p], mate_id)

    def own_out(i, p):
        dst = (dq_ref, dk_ref, dv_ref)[i].at[span(core * half, p)]
        return pltpu.make_async_copy(staged(i, core, p), dst, loc_out.at[i, p])

    def each(body):
        lax.fori_loop(0, pieces, lambda p, carry: (body(p), carry)[1], 0)

    barrier = pltpu.get_barrier_semaphore()
    pl.semaphore_signal(barrier, inc=1, device_id=mate_id, device_id_type=MESH)

    @pl.when(paired)
    def _():
        for j in range(2):
            pl.semaphore_signal(barrier, inc=1, device_id=device(other_chip, j), device_id_type=MESH)

    @pl.when(chained)
    def _():
        single = jnp.where(is_left, ahead_relay, back_relay)
        double = jnp.where(is_left, back_relay, ahead_relay)
        for to in (device(single, core), device(double, 0), device(double, 1)):
            pl.semaphore_signal(barrier, inc=1, device_id=to, device_id_type=MESH)
        pl.semaphore_wait(barrier, 6)

    @pl.when(relays)
    def _():
        for f in range(flows):
            single, double = relay_ends(f)
            for to in (device(single, core), device(double, 0), device(double, 1)):
                pl.semaphore_signal(barrier, inc=1, device_id=to, device_id_type=MESH)

    @pl.when(relays & paired)
    def _():
        pl.semaphore_wait(barrier, 3 + 3 * flows)

    @pl.when(relays & jnp.logical_not(paired))
    def _():
        pl.semaphore_wait(barrier, 1 + 3 * flows)

    @pl.when(is_left)
    def _():
        def send(p):
            for j in range(2):
                for i in range(2):
                    ahead(i, j, p).start()

        @pl.when(chained)
        def _():
            for r in range(DETOUR):
                for j in range(2):
                    for i in range(2):
                        ahead_detour(i, j, r).start()

        lax.fori_loop(0, pieces - DETOUR, lambda p, carry: (send(p), carry)[1], 0)

        @pl.when(jnp.logical_not(chained))
        def _():
            for r in range(DETOUR):
                send(pieces - DETOUR + r)

    doc_copy().start()
    for i in range(3):
        own_in(i).start()

    def send_mate(p):
        for i in range(3):
            mate_in(i, p).start()

    each(send_mate)
    dbuf[core] = doc_ref[...]
    for i in range(3):
        own_in(i).wait()
    doc_copy().wait_send()
    remote(doc_ref, dbuf.at[mate], doc_s.at[0], doc_r.at[0], mate_id).wait_recv()

    wide = 2 * toks
    base = chip * wide
    first = jnp.concatenate([dbuf[0], dbuf[1]], axis=1)
    query_pos = base + lax.broadcasted_iota(jnp.int32, (2 * wide, wide), 1)
    key_pos = base - wide + lax.broadcasted_iota(jnp.int32, (2 * wide, wide), 0)
    bias[...] = jnp.where((key_pos >= first) & (key_pos <= query_pos), 0.0, -jnp.inf)

    def one_head(h, slots):
        query = jnp.concatenate([qbuf[0, h], qbuf[1, h]], axis=1)
        key = jnp.concatenate([kvbuf[0, s, h] for s in slots], axis=1)
        value = jnp.concatenate([kvbuf[1, s, h] for s in slots], axis=1)
        rows = pl.ds(slots[0] * toks, len(slots) * toks)
        dot = functools.partial(lax.dot_general, preferred_element_type=jnp.float32)
        tn, nn, nt = ((((0,), (0,)), ((), ())), (((1,), (0,)), ((), ())), (((1,), (1,)), ((), ())))
        scores = dot(key, query, tn) * (scale * math.log2(math.e)) + bias[rows, :]
        weights = jnp.exp2(scores - jnp.max(scores, axis=0, keepdims=True))
        probs = weights * (1.0 / jnp.sum(weights, axis=0, keepdims=True))
        low = probs.astype(jnp.bfloat16)
        attended = dot(value, low, nn).astype(jnp.bfloat16)
        wide_att = attended.astype(jnp.float32)
        row_dot = jnp.sum(wide_att * wide_att, axis=0, keepdims=True)
        grad_probs = dot(value, attended, tn)
        grad_scores = (probs * (grad_probs - row_dot)).astype(jnp.bfloat16)
        grad_q = (dot(key, grad_scores, nn) * scale).astype(jnp.bfloat16)
        grad_k = (dot(query, grad_scores, nt) * scale).astype(jnp.bfloat16)
        grad_v = dot(attended, low, nt).astype(jnp.bfloat16)
        for j in range(2):
            stage_q[j, h] = grad_q[:, j * toks : (j + 1) * toks]
        for n, s in enumerate(slots):
            stage_kv[0, s, h] = grad_k[:, n * toks : (n + 1) * toks]
            stage_kv[1, s, h] = grad_v[:, n * toks : (n + 1) * toks]

    def work(p, slots):
        for i in range(3):
            dst = qbuf.at[mate, span(0, p)] if i == 0 else kvbuf.at[i - 1, 2 + mate, span(0, p)]
            src = (q_ref, k_ref, v_ref)[i].at[span(mate * half, p)]
            remote(src, dst, in_s.at[i, p], in_r.at[i, p], mate_id).wait_recv()
        for n in range(PIECE):
            one_head(p * PIECE + n, slots)
        for i in range(3):
            mate_out(i, p).start()
            own_out(i, p).start()

    @pl.when(is_right)
    def _():
        def send_back(p):
            for j in range(2):
                for i in range(2):
                    back(i, j, p).start()

        def send_most():
            for r in range(DETOUR):
                for j in range(2):
                    for i in range(2):
                        back_detour(i, j, r).start()
            lax.fori_loop(DETOUR, pieces - 1, lambda e, carry: (send_back(e), carry)[1], 0)

        def step(p):
            for j in range(2):
                for i in range(2):
                    ahead_arrival(i, j, p).wait_recv()

            @pl.when(chained & (p == pieces - 1))
            def _():
                send_most()

            work(p, (0, 1, 2, 3))

            @pl.when(jnp.logical_not(chained))
            def _():
                send_back(p)

                @pl.when(p < items)
                def _():
                    relay(ahead_onward, p)

        each(step)

        @pl.when(chained)
        def _():
            send_back(pieces - 1)

    @pl.when(jnp.logical_not(is_right))
    def _():
        def step(p):
            work(p, (2, 3))

            @pl.when((chip == last) & (p < items))
            def _():
                relay(ahead_onward, p)

        each(step)

    def drain(p):
        for i in range(3):
            mate_in(i, p).wait_send()
            own_out(i, p).wait()
            mate_out(i, p).wait_send()
            mate_out_arrival(i, p).wait_recv()

    each(drain)

    @pl.when(relays_back)
    def _():
        lax.fori_loop(0, items, lambda t, carry: (relay(back_onward, t), carry)[1], 0)

    @pl.when(is_left)
    def _():
        def add(p):
            for i in range(2):
                out = (dk_ref, dv_ref)[i]
                for j in range(2):
                    ahead(i, j, p).wait_send()
                    back_arrival(i, j, p).wait_recv()
                    at = span(j * half, p)
                    total = out[at].astype(jnp.float32) + part[i, j, span(0, p)].astype(jnp.float32)
                    out[at] = total.astype(jnp.bfloat16)

        each(add)

    @pl.when(is_right)
    def _():
        def sent(p):
            for j in range(2):
                for i in range(2):
                    back(i, j, p).wait_send()

        each(sent)

    @pl.when(relays)
    def _():
        def onward_sent(t):
            for j in range(2):
                for i in range(2):
                    ahead_onward(t % flows, i, j, t // flows).wait_send()

        lax.fori_loop(0, items, lambda t, carry: (onward_sent(t), carry)[1], 0)


def chunk_shards(n_ctx, n_head, queries, keys, values, doc_start):
    heads, depth, toks = queries.shape
    half = heads // 2
    pieces = half // PIECE
    like = jax.ShapeDtypeStruct(queries.shape, jnp.bfloat16)
    vmem = pl.BlockSpec(memory_space=pltpu.VMEM)
    low, sem = jnp.bfloat16, pltpu.SemaphoreType.DMA
    return pl.pallas_call(
        functools.partial(chunk_kernel, n_ctx, n_head),
        out_shape=(like, like, like),
        in_specs=[pl.BlockSpec(memory_space=pltpu.HBM)] * 3 + [vmem],
        out_specs=(vmem,) * 3,
        scratch_shapes=[
            pltpu.VMEM((2, half, depth, toks), low),
            pltpu.VMEM((2, 4, half, depth, toks), low),
            pltpu.VMEM((2, 1, toks), jnp.int32),
            pltpu.VMEM((4 * toks, 2 * toks), jnp.float32),
            pltpu.VMEM((2, half, depth, toks), low),
            pltpu.VMEM((2, 4, half, depth, toks), low),
            pltpu.VMEM((2, 2, half, depth, toks), low),
            sem((3, pieces)), sem((3, pieces)), sem((3,)), sem((1,)), sem((1,)),
            sem((2, 2, pieces)), sem((2, 2, pieces)), sem((2, 2, pieces)), sem((2, 2, pieces)),
            sem((3, pieces)), sem((3, pieces)), sem((3, pieces)),
            pltpu.VMEM((n_ctx - 1, 2, 2, DETOUR, PIECE, depth, toks), low),
            sem((n_ctx - 1, 2, 2, DETOUR)), sem((n_ctx - 1, 2, 2, DETOUR)),
        ],
        compiler_params=pltpu.CompilerParams(
            collective_id=0, has_side_effects=True, vmem_limit_bytes=60 * 1024 * 1024
        ),
        cost_estimate=pl.CostEstimate(
            flops=12 * half * 8 * toks * toks * depth, bytes_accessed=12 * heads * depth * toks,
            transcendentals=8 * half * toks * toks,
        ),
    )(queries, keys, values, doc_start.reshape(1, toks))


def solution(mesh):
    n_ctx, n_head = mesh.shape["ctx"], mesh.shape["head"]

    def program(queries, keys, values, doc_start):
        toks = queries.shape[2]
        pieces = queries.shape[0] // (2 * PIECE)
        fits = queries.shape[0] % (2 * PIECE) == 0 and 1 < n_ctx and (n_ctx - 1) * DETOUR <= pieces
        if 4 * toks == DOC_MAX and n_head * toks == 2 * DOC_MAX and fits:
            return chunk_shards(n_ctx, n_head, queries, keys, values, doc_start)
        return shards(queries, keys, values, doc_start)

    spec = P(None, None, ("ctx", "head"))
    return jax.shard_map(
        program,
        mesh=mesh,
        in_specs=(spec, spec, spec, P(("ctx", "head"))),
        out_specs=(spec, spec, spec),
        check_vma=False,
    )
```

```python
import functools
import math

import jax
import jax.numpy as jnp
from jax import lax
from jax.experimental import pallas as pl
from jax.experimental.pallas import tpu as pltpu
from jax.sharding import PartitionSpec as P

DOC_MAX = 512
PIECE = 1
STEP = 2
DETOUR = 3
MESH = pl.DeviceIdType.MESH


def from_behind(value, axis, steps):
    count = lax.axis_size(axis)
    first, last = (max(0, -steps), min(count, count - steps))
    return lax.ppermute(value, axis, [(source, source + steps) for source in range(first, last)])


def block_grads(query_blk, key_win, value_win, first_pos, query_pos, key_pos, score_scale):
    visible = (key_pos[None, :] >= first_pos[:, None]) & (key_pos[None, :] <= query_pos[:, None])
    scores = (
        jnp.einsum("hdq,hdk->hqk", query_blk, key_win, preferred_element_type=jnp.float32)
        * score_scale
    )
    scores = jnp.where(visible[None], scores, -jnp.inf)
    row_peak = jnp.max(scores, axis=2, keepdims=True)
    weights = jnp.exp(scores - row_peak)
    soft_probs = weights / jnp.sum(weights, axis=2, keepdims=True)
    probs_low = soft_probs.astype(jnp.bfloat16)
    attended = jnp.einsum(
        "hqk,hdk->hdq", probs_low, value_win, preferred_element_type=jnp.float32
    ).astype(jnp.bfloat16)
    grad_value = jnp.einsum("hqk,hdq->hdk", probs_low, attended, preferred_element_type=jnp.float32)
    grad_probs = jnp.einsum("hdq,hdk->hqk", attended, value_win, preferred_element_type=jnp.float32)
    wide_att = attended.astype(jnp.float32)
    row_dot = jnp.sum(wide_att * wide_att, axis=1)
    grad_scores = (soft_probs * (grad_probs - row_dot[:, :, None])).astype(jnp.bfloat16)
    grad_query = (
        jnp.einsum("hqk,hdk->hdq", grad_scores, key_win, preferred_element_type=jnp.float32)
        * score_scale
    ).astype(jnp.bfloat16)
    grad_key = jnp.einsum(
        "hqk,hdq->hdk", grad_scores, query_blk, preferred_element_type=jnp.float32
    )
    return (grad_query, grad_key, grad_value)


def shards(queries, keys, values, doc_start):
    score_scale = 1.0 / math.sqrt(queries.shape[1])
    head_q, head_k, head_v = (
        lax.all_to_all(queries, "head", split_axis=0, concat_axis=2, tiled=True),
        lax.all_to_all(keys, "head", split_axis=0, concat_axis=2, tiled=True),
        lax.all_to_all(values, "head", split_axis=0, concat_axis=2, tiled=True),
    )
    starts = lax.all_gather(doc_start, "head", axis=0, tiled=True)
    local_heads = head_q.shape[0]
    head_depth = head_q.shape[1]
    group_span = head_q.shape[2]
    window = DOC_MAX
    blocks = group_span // window
    prior_k, prior_v = from_behind(
        (head_k[:, :, group_span - window :], head_v[:, :, group_span - window :]), "ctx", 1
    )
    anchor = lax.axis_index("ctx") * group_span
    key_ext = jnp.concatenate([prior_k, head_k], axis=2).reshape(
        local_heads, head_depth, blocks + 1, window
    )
    value_ext = jnp.concatenate([prior_v, head_v], axis=2).reshape(
        local_heads, head_depth, blocks + 1, window
    )
    key_wins = jnp.moveaxis(jnp.concatenate([key_ext[:, :, :-1], key_ext[:, :, 1:]], axis=3), 2, 0)
    value_wins = jnp.moveaxis(
        jnp.concatenate([value_ext[:, :, :-1], value_ext[:, :, 1:]], axis=3), 2, 0
    )
    query_blocks = jnp.moveaxis(head_q.reshape(local_heads, head_depth, blocks, window), 2, 0)
    start_blocks = starts.reshape(blocks, window)
    offsets = jnp.arange(window, dtype=jnp.int32)
    spread = jnp.arange(2 * window, dtype=jnp.int32)

    def one_block(unused_carry, block_item):
        query_blk, key_win, value_win, first_pos, number = block_item
        block_base = anchor + number * window
        query_pos = block_base + offsets
        key_pos = block_base - window + spread
        return (
            unused_carry,
            block_grads(query_blk, key_win, value_win, first_pos, query_pos, key_pos, score_scale),
        )

    _, (query_stack, key_stack, value_stack) = lax.scan(
        one_block,
        jnp.int32(0),
        (query_blocks, key_wins, value_wins, start_blocks, jnp.arange(blocks, dtype=jnp.int32)),
    )
    far_k = key_stack[..., :window]
    far_v = value_stack[..., :window]
    own_k = key_stack[..., window:] + jnp.concatenate(
        [far_k[1:], jnp.zeros_like(far_k[:1])], axis=0
    )
    own_v = value_stack[..., window:] + jnp.concatenate(
        [far_v[1:], jnp.zeros_like(far_v[:1])], axis=0
    )
    back_k, back_v = from_behind((far_k[0], far_v[0]), "ctx", -1)
    own_k = own_k.at[blocks - 1].add(back_k)
    own_v = own_v.at[blocks - 1].add(back_v)

    def to_span(stacked):
        return jnp.moveaxis(stacked, 0, 2).reshape(local_heads, head_depth, group_span)

    grad_q = to_span(query_stack)
    grad_k = (to_span(own_k) * score_scale).astype(jnp.bfloat16)
    grad_v = to_span(own_v).astype(jnp.bfloat16)
    return (
        lax.all_to_all(grad_q, "head", split_axis=2, concat_axis=0, tiled=True),
        lax.all_to_all(grad_k, "head", split_axis=2, concat_axis=0, tiled=True),
        lax.all_to_all(grad_v, "head", split_axis=2, concat_axis=0, tiled=True),
    )


def chunk_kernel(
    n_ctx, n_head, q_ref, k_ref, v_ref, doc_ref, dq_ref, dk_ref, dv_ref,
    qbuf, kvbuf, dbuf, bias, stage_q, stage_kv, part,
    in_s, in_r, loc_in, doc_s, doc_r, l_s, l_r, g_s, g_r, o_s, o_r, loc_out, rbuf, r_s, r_r,
):
    heads, depth, toks = q_ref.shape
    half = heads // 2
    pieces = half // PIECE
    scale = 1.0 / math.sqrt(depth)
    me = lax.axis_index("ctx") * n_head + lax.axis_index("head")
    chip, core = me // 2, me % 2
    mate = 1 - core
    last = n_ctx * n_head // 2 - 1
    odd = chip % 2
    is_left = (chip == 0) | ((odd == 1) & (chip >= 3) & (chip < last))
    is_right = (chip == 1) | ((odd == 0) & (chip >= 4))
    paired = is_left | is_right
    other_chip = jnp.where(is_left, chip + 1, chip - 1)

    flows = n_ctx - 1
    items = flows * DETOUR
    chained = paired & (chip >= 3)
    flow = (chip + 1) // 4 - 1
    far = (chip + 1) % 4 < 2
    ahead_relay, back_relay = jnp.where(far, last, 1), jnp.where(far, 0, 2)
    relays_ahead = (chip == last) | (chip == 1)
    relays_back = (chip == 0) | (chip == 2)
    relays = relays_ahead | relays_back
    far_relay = (chip == last) | (chip == 0)

    def relay_ends(f):
        left = 4 * f + 4 + jnp.where(far_relay, -1, 1)
        return jnp.where(relays_ahead, left, left + 1), jnp.where(relays_ahead, left + 1, left)

    def device(chip_id, core_id):
        linear = chip_id * 2 + core_id
        return (linear // n_head, linear % n_head)

    mate_id = device(chip, mate)

    def remote(src, dst, send, recv, to):
        return pltpu.make_async_remote_copy(
            src_ref=src, dst_ref=dst, send_sem=send, recv_sem=recv, device_id=to, device_id_type=MESH
        )

    def span(base, p):
        return pl.ds(base + p * PIECE, PIECE)

    def mate_in(i, p):
        src = (q_ref, k_ref, v_ref)[i].at[span(mate * half, p)]
        dst = qbuf.at[core, span(0, p)] if i == 0 else kvbuf.at[i - 1, 2 + core, span(0, p)]
        return remote(src, dst, in_s.at[i, p], in_r.at[i, p], mate_id)

    def own_in(i):
        src = (q_ref, k_ref, v_ref)[i].at[pl.ds(core * half, half)]
        dst = qbuf.at[core] if i == 0 else kvbuf.at[i - 1, 2 + core]
        return pltpu.make_async_copy(src, dst, loc_in.at[i])

    def doc_copy():
        return remote(doc_ref, dbuf.at[core], doc_s.at[0], doc_r.at[0], mate_id)

    def ahead(i, j, p):
        src = (k_ref, v_ref)[i].at[span(j * half, p)]
        return remote(
            src, kvbuf.at[i, core, span(0, p)], l_s.at[i, j, p], l_r.at[i, core, p], device(other_chip, j)
        )

    def ahead_arrival(i, j, p):
        src = (k_ref, v_ref)[i].at[span(j * half, p)]
        return remote(
            src, kvbuf.at[i, j, span(0, p)], l_s.at[i, j, p], l_r.at[i, j, p], device(other_chip, j)
        )

    def back(i, j, p):
        return remote(
            stage_kv.at[i, j, span(0, p)], part.at[i, core, span(0, p)],
            g_s.at[i, j, p], g_r.at[i, core, p], device(other_chip, j),
        )

    def back_arrival(i, j, p):
        return remote(
            stage_kv.at[i, j, span(0, p)], part.at[i, j, span(0, p)],
            g_s.at[i, j, p], g_r.at[i, j, p], device(other_chip, j),
        )

    def ahead_detour(i, j, r):
        p = pieces - DETOUR + r
        src = (k_ref, v_ref)[i].at[span(j * half, p)]
        return remote(
            src, rbuf.at[flow, i, j, r], l_s.at[i, j, p], r_r.at[flow, i, j, r], device(ahead_relay, core)
        )

    def back_detour(i, j, r):
        return remote(
            stage_kv.at[i, j, span(0, r)], rbuf.at[flow, i, j, r],
            g_s.at[i, j, r], r_r.at[flow, i, j, r], device(back_relay, core),
        )

    def detour_arrival(f, i, j, r):
        return remote(
            rbuf.at[f, i, j, r], rbuf.at[f, i, j, r], r_s.at[f, i, j, r], r_r.at[f, i, j, r],
            device(relay_ends(f)[1], j),
        )

    def ahead_onward(f, i, j, r):
        p = pieces - DETOUR + r
        return remote(
            rbuf.at[f, i, j, r], kvbuf.at[i, core, span(0, p)],
            r_s.at[f, i, j, r], l_r.at[i, core, p], device(relay_ends(f)[1], j),
        )

    def back_onward(f, i, j, r):
        return remote(
            rbuf.at[f, i, j, r], part.at[i, core, span(0, r)],
            r_s.at[f, i, j, r], g_r.at[i, core, r], device(relay_ends(f)[1], j),
        )

    def relay(onward, item):
        f, r = item % flows, item // flows
        for j in range(2):
            for i in range(2):
                detour_arrival(f, i, j, r).wait_recv()
                onward(f, i, j, r).start()

    def staged(i, whose, p):
        return stage_q.at[whose, span(0, p)] if i == 0 else stage_kv.at[i - 1, 2 + whose, span(0, p)]

    def mate_out(i, p):
        dst = (dq_ref, dk_ref, dv_ref)[i].at[span(core * half, p)]
        return remote(staged(i, mate, p), dst, o_s.at[i, p], o_r.at[i, p], mate_id)

    def mate_out_arrival(i, p):
        dst = (dq_ref, dk_ref, dv_ref)[i].at[span(mate * half, p)]
        return remote(staged(i, mate, p), dst, o_s.at[i, p], o_r.at[i, p], mate_id)

    def own_out(i, p):
        dst = (dq_ref, dk_ref, dv_ref)[i].at[span(core * half, p)]
        return pltpu.make_async_copy(staged(i, core, p), dst, loc_out.at[i, p])

    def each_step(body):
        lax.fori_loop(0, pieces // STEP, lambda t, carry: (body(t), carry)[1], 0)

    def each(body):
        lax.fori_loop(0, pieces, lambda p, carry: (body(p), carry)[1], 0)

    barrier = pltpu.get_barrier_semaphore()
    pl.semaphore_signal(barrier, inc=1, device_id=mate_id, device_id_type=MESH)

    @pl.when(paired)
    def _():
        for j in range(2):
            pl.semaphore_signal(barrier, inc=1, device_id=device(other_chip, j), device_id_type=MESH)

    @pl.when(chained)
    def _():
        single = jnp.where(is_left, ahead_relay, back_relay)
        double = jnp.where(is_left, back_relay, ahead_relay)
        for to in (device(single, core), device(double, 0), device(double, 1)):
            pl.semaphore_signal(barrier, inc=1, device_id=to, device_id_type=MESH)
        pl.semaphore_wait(barrier, 6)

    @pl.when(relays)
    def _():
        for f in range(flows):
            single, double = relay_ends(f)
            for to in (device(single, core), device(double, 0), device(double, 1)):
                pl.semaphore_signal(barrier, inc=1, device_id=to, device_id_type=MESH)

    @pl.when(relays & paired)
    def _():
        pl.semaphore_wait(barrier, 3 + 3 * flows)

    @pl.when(relays & jnp.logical_not(paired))
    def _():
        pl.semaphore_wait(barrier, 1 + 3 * flows)

    @pl.when(is_left)
    def _():
        def send(p):
            for j in range(2):
                for i in range(2):
                    ahead(i, j, p).start()

        @pl.when(chained)
        def _():
            for r in range(DETOUR):
                for j in range(2):
                    for i in range(2):
                        ahead_detour(i, j, r).start()

        lax.fori_loop(0, pieces - DETOUR, lambda p, carry: (send(p), carry)[1], 0)

        @pl.when(jnp.logical_not(chained))
        def _():
            for r in range(DETOUR):
                send(pieces - DETOUR + r)

    doc_copy().start()
    for i in range(3):
        own_in(i).start()

    def send_mate(p):
        for i in range(3):
            mate_in(i, p).start()

    each(send_mate)
    dbuf[core] = doc_ref[...]
    for i in range(3):
        own_in(i).wait()
    doc_copy().wait_send()
    remote(doc_ref, dbuf.at[mate], doc_s.at[0], doc_r.at[0], mate_id).wait_recv()

    wide = 2 * toks
    base = chip * wide
    first = jnp.concatenate([dbuf[0], dbuf[1]], axis=1)
    query_pos = base + lax.broadcasted_iota(jnp.int32, (2 * wide, wide), 1)
    key_pos = base - wide + lax.broadcasted_iota(jnp.int32, (2 * wide, wide), 0)
    bias[...] = jnp.where((key_pos >= first) & (key_pos <= query_pos), 0.0, -jnp.inf)

    def one_head(h, slots):
        query = jnp.concatenate([qbuf[0, h], qbuf[1, h]], axis=1)
        key = jnp.concatenate([kvbuf[0, s, h] for s in slots], axis=1)
        value = jnp.concatenate([kvbuf[1, s, h] for s in slots], axis=1)
        rows = pl.ds(slots[0] * toks, len(slots) * toks)
        dot = functools.partial(lax.dot_general, preferred_element_type=jnp.float32)
        tn, nn, nt = ((((0,), (0,)), ((), ())), (((1,), (0,)), ((), ())), (((1,), (1,)), ((), ())))
        scores = dot(key, query, tn) * (scale * math.log2(math.e)) + bias[rows, :]
        weights = jnp.exp2(scores - jnp.max(scores, axis=0, keepdims=True))
        probs = weights * (1.0 / jnp.sum(weights, axis=0, keepdims=True))
        low = probs.astype(jnp.bfloat16)
        attended = dot(value, low, nn).astype(jnp.bfloat16)
        wide_att = attended.astype(jnp.float32)
        row_dot = jnp.sum(wide_att * wide_att, axis=0, keepdims=True)
        grad_probs = dot(value, attended, tn)
        grad_scores = (probs * (grad_probs - row_dot)).astype(jnp.bfloat16)
        grad_q = (dot(key, grad_scores, nn) * scale).astype(jnp.bfloat16)
        grad_k = (dot(query, grad_scores, nt) * scale).astype(jnp.bfloat16)
        grad_v = dot(attended, low, nt).astype(jnp.bfloat16)
        for j in range(2):
            stage_q[j, h] = grad_q[:, j * toks : (j + 1) * toks]
        for n, s in enumerate(slots):
            stage_kv[0, s, h] = grad_k[:, n * toks : (n + 1) * toks]
            stage_kv[1, s, h] = grad_v[:, n * toks : (n + 1) * toks]

    def work(t, slots):
        for n in range(STEP):
            p = t * STEP + n
            for i in range(3):
                dst = qbuf.at[mate, span(0, p)] if i == 0 else kvbuf.at[i - 1, 2 + mate, span(0, p)]
                src = (q_ref, k_ref, v_ref)[i].at[span(mate * half, p)]
                remote(src, dst, in_s.at[i, p], in_r.at[i, p], mate_id).wait_recv()
        for n in range(STEP * PIECE):
            one_head(t * STEP * PIECE + n, slots)
        for n in range(STEP):
            for i in range(3):
                mate_out(i, t * STEP + n).start()
                own_out(i, t * STEP + n).start()

    def relay_step(t):
        for n in range(STEP):
            @pl.when(t * STEP + n < items)
            def _():
                relay(ahead_onward, t * STEP + n)

    @pl.when(is_right)
    def _():
        def send_back(p):
            for j in range(2):
                for i in range(2):
                    back(i, j, p).start()

        def send_detour(r):
            for j in range(2):
                for i in range(2):
                    back_detour(i, j, r).start()

        def send_most():
            @pl.when(jnp.logical_not(far))
            def _():
                for r in range(DETOUR):
                    send_detour(r)

            lax.fori_loop(DETOUR, pieces - STEP, lambda e, carry: (send_back(e), carry)[1], 0)

        def step(t):
            for n in range(STEP):
                for j in range(2):
                    for i in range(2):
                        ahead_arrival(i, j, t * STEP + n).wait_recv()

            @pl.when(chained & (t == pieces // STEP - 1))
            def _():
                send_most()

            work(t, (0, 1, 2, 3))

            for n in range(STEP):
                @pl.when(chained & far & (t * STEP + n < DETOUR))
                def _():
                    send_detour(t * STEP + n)

            @pl.when(jnp.logical_not(chained))
            def _():
                for n in range(STEP):
                    send_back(t * STEP + n)
                relay_step(t)

        each_step(step)

        @pl.when(chained)
        def _():
            for n in range(STEP):
                send_back(pieces - STEP + n)

    @pl.when(jnp.logical_not(is_right))
    def _():
        def step(t):
            work(t, (2, 3))

            @pl.when(chip == last)
            def _():
                relay_step(t)

        each_step(step)

    def drain(p):
        for i in range(3):
            mate_in(i, p).wait_send()
            own_out(i, p).wait()
            mate_out(i, p).wait_send()
            mate_out_arrival(i, p).wait_recv()

    each(drain)

    @pl.when(relays_back)
    def _():
        lax.fori_loop(0, items, lambda t, carry: (relay(back_onward, t), carry)[1], 0)

    @pl.when(is_left)
    def _():
        def add(p):
            for i in range(2):
                out = (dk_ref, dv_ref)[i]
                for j in range(2):
                    ahead(i, j, p).wait_send()
                    back_arrival(i, j, p).wait_recv()
                    at = span(j * half, p)
                    total = out[at].astype(jnp.float32) + part[i, j, span(0, p)].astype(jnp.float32)
                    out[at] = total.astype(jnp.bfloat16)

        each(add)

    @pl.when(is_right)
    def _():
        def sent(p):
            for j in range(2):
                for i in range(2):
                    back(i, j, p).wait_send()

        each(sent)

    @pl.when(relays)
    def _():
        def onward_sent(t):
            for j in range(2):
                for i in range(2):
                    ahead_onward(t % flows, i, j, t // flows).wait_send()

        lax.fori_loop(0, items, lambda t, carry: (onward_sent(t), carry)[1], 0)


def chunk_shards(n_ctx, n_head, queries, keys, values, doc_start):
    heads, depth, toks = queries.shape
    half = heads // 2
    pieces = half // PIECE
    like = jax.ShapeDtypeStruct(queries.shape, jnp.bfloat16)
    vmem = pl.BlockSpec(memory_space=pltpu.VMEM)
    low, sem = jnp.bfloat16, pltpu.SemaphoreType.DMA
    return pl.pallas_call(
        functools.partial(chunk_kernel, n_ctx, n_head),
        out_shape=(like, like, like),
        in_specs=[pl.BlockSpec(memory_space=pltpu.HBM)] * 3 + [vmem],
        out_specs=(vmem,) * 3,
        scratch_shapes=[
            pltpu.VMEM((2, half, depth, toks), low),
            pltpu.VMEM((2, 4, half, depth, toks), low),
            pltpu.VMEM((2, 1, toks), jnp.int32),
            pltpu.VMEM((4 * toks, 2 * toks), jnp.float32),
            pltpu.VMEM((2, half, depth, toks), low),
            pltpu.VMEM((2, 4, half, depth, toks), low),
            pltpu.VMEM((2, 2, half, depth, toks), low),
            sem((3, pieces)), sem((3, pieces)), sem((3,)), sem((1,)), sem((1,)),
            sem((2, 2, pieces)), sem((2, 2, pieces)), sem((2, 2, pieces)), sem((2, 2, pieces)),
            sem((3, pieces)), sem((3, pieces)), sem((3, pieces)),
            pltpu.VMEM((n_ctx - 1, 2, 2, DETOUR, PIECE, depth, toks), low),
            sem((n_ctx - 1, 2, 2, DETOUR)), sem((n_ctx - 1, 2, 2, DETOUR)),
        ],
        compiler_params=pltpu.CompilerParams(
            collective_id=0, has_side_effects=True, vmem_limit_bytes=60 * 1024 * 1024
        ),
        cost_estimate=pl.CostEstimate(
            flops=12 * half * 8 * toks * toks * depth, bytes_accessed=12 * heads * depth * toks,
            transcendentals=8 * half * toks * toks,
        ),
    )(queries, keys, values, doc_start.reshape(1, toks))


def solution(mesh):
    n_ctx, n_head = mesh.shape["ctx"], mesh.shape["head"]

    def program(queries, keys, values, doc_start):
        toks = queries.shape[2]
        pieces = queries.shape[0] // (2 * PIECE)
        fits = queries.shape[0] % (2 * PIECE * STEP) == 0 and 1 < n_ctx and (n_ctx - 1) * DETOUR <= pieces - STEP
        if 4 * toks == DOC_MAX and n_head * toks == 2 * DOC_MAX and fits:
            return chunk_shards(n_ctx, n_head, queries, keys, values, doc_start)
        return shards(queries, keys, values, doc_start)

    spec = P(None, None, ("ctx", "head"))
    return jax.shard_map(
        program,
        mesh=mesh,
        in_specs=(spec, spec, spec, P(("ctx", "head"))),
        out_specs=(spec, spec, spec),
        check_vma=False,
    )
```

```python
import functools
import math

import jax
import jax.numpy as jnp
from jax import lax
from jax.experimental import pallas as pl
from jax.experimental.pallas import tpu as pltpu
from jax.sharding import PartitionSpec as P

DOC_MAX = 512
PIECE = 1
STEP = 2
DETOUR = 3
MESH = pl.DeviceIdType.MESH


def from_behind(value, axis, steps):
    count = lax.axis_size(axis)
    first, last = (max(0, -steps), min(count, count - steps))
    return lax.ppermute(value, axis, [(source, source + steps) for source in range(first, last)])


def block_grads(query_blk, key_win, value_win, first_pos, query_pos, key_pos, score_scale):
    visible = (key_pos[None, :] >= first_pos[:, None]) & (key_pos[None, :] <= query_pos[:, None])
    scores = (
        jnp.einsum("hdq,hdk->hqk", query_blk, key_win, preferred_element_type=jnp.float32)
        * score_scale
    )
    scores = jnp.where(visible[None], scores, -jnp.inf)
    row_peak = jnp.max(scores, axis=2, keepdims=True)
    weights = jnp.exp(scores - row_peak)
    soft_probs = weights / jnp.sum(weights, axis=2, keepdims=True)
    probs_low = soft_probs.astype(jnp.bfloat16)
    attended = jnp.einsum(
        "hqk,hdk->hdq", probs_low, value_win, preferred_element_type=jnp.float32
    ).astype(jnp.bfloat16)
    grad_value = jnp.einsum("hqk,hdq->hdk", probs_low, attended, preferred_element_type=jnp.float32)
    grad_probs = jnp.einsum("hdq,hdk->hqk", attended, value_win, preferred_element_type=jnp.float32)
    wide_att = attended.astype(jnp.float32)
    row_dot = jnp.sum(wide_att * wide_att, axis=1)
    grad_scores = (soft_probs * (grad_probs - row_dot[:, :, None])).astype(jnp.bfloat16)
    grad_query = (
        jnp.einsum("hqk,hdk->hdq", grad_scores, key_win, preferred_element_type=jnp.float32)
        * score_scale
    ).astype(jnp.bfloat16)
    grad_key = jnp.einsum(
        "hqk,hdq->hdk", grad_scores, query_blk, preferred_element_type=jnp.float32
    )
    return (grad_query, grad_key, grad_value)


def shards(queries, keys, values, doc_start):
    score_scale = 1.0 / math.sqrt(queries.shape[1])
    head_q, head_k, head_v = (
        lax.all_to_all(queries, "head", split_axis=0, concat_axis=2, tiled=True),
        lax.all_to_all(keys, "head", split_axis=0, concat_axis=2, tiled=True),
        lax.all_to_all(values, "head", split_axis=0, concat_axis=2, tiled=True),
    )
    starts = lax.all_gather(doc_start, "head", axis=0, tiled=True)
    local_heads = head_q.shape[0]
    head_depth = head_q.shape[1]
    group_span = head_q.shape[2]
    window = DOC_MAX
    blocks = group_span // window
    prior_k, prior_v = from_behind(
        (head_k[:, :, group_span - window :], head_v[:, :, group_span - window :]), "ctx", 1
    )
    anchor = lax.axis_index("ctx") * group_span
    key_ext = jnp.concatenate([prior_k, head_k], axis=2).reshape(
        local_heads, head_depth, blocks + 1, window
    )
    value_ext = jnp.concatenate([prior_v, head_v], axis=2).reshape(
        local_heads, head_depth, blocks + 1, window
    )
    key_wins = jnp.moveaxis(jnp.concatenate([key_ext[:, :, :-1], key_ext[:, :, 1:]], axis=3), 2, 0)
    value_wins = jnp.moveaxis(
        jnp.concatenate([value_ext[:, :, :-1], value_ext[:, :, 1:]], axis=3), 2, 0
    )
    query_blocks = jnp.moveaxis(head_q.reshape(local_heads, head_depth, blocks, window), 2, 0)
    start_blocks = starts.reshape(blocks, window)
    offsets = jnp.arange(window, dtype=jnp.int32)
    spread = jnp.arange(2 * window, dtype=jnp.int32)

    def one_block(unused_carry, block_item):
        query_blk, key_win, value_win, first_pos, number = block_item
        block_base = anchor + number * window
        query_pos = block_base + offsets
        key_pos = block_base - window + spread
        return (
            unused_carry,
            block_grads(query_blk, key_win, value_win, first_pos, query_pos, key_pos, score_scale),
        )

    _, (query_stack, key_stack, value_stack) = lax.scan(
        one_block,
        jnp.int32(0),
        (query_blocks, key_wins, value_wins, start_blocks, jnp.arange(blocks, dtype=jnp.int32)),
    )
    far_k = key_stack[..., :window]
    far_v = value_stack[..., :window]
    own_k = key_stack[..., window:] + jnp.concatenate(
        [far_k[1:], jnp.zeros_like(far_k[:1])], axis=0
    )
    own_v = value_stack[..., window:] + jnp.concatenate(
        [far_v[1:], jnp.zeros_like(far_v[:1])], axis=0
    )
    back_k, back_v = from_behind((far_k[0], far_v[0]), "ctx", -1)
    own_k = own_k.at[blocks - 1].add(back_k)
    own_v = own_v.at[blocks - 1].add(back_v)

    def to_span(stacked):
        return jnp.moveaxis(stacked, 0, 2).reshape(local_heads, head_depth, group_span)

    grad_q = to_span(query_stack)
    grad_k = (to_span(own_k) * score_scale).astype(jnp.bfloat16)
    grad_v = to_span(own_v).astype(jnp.bfloat16)
    return (
        lax.all_to_all(grad_q, "head", split_axis=2, concat_axis=0, tiled=True),
        lax.all_to_all(grad_k, "head", split_axis=2, concat_axis=0, tiled=True),
        lax.all_to_all(grad_v, "head", split_axis=2, concat_axis=0, tiled=True),
    )


def chunk_kernel(
    n_ctx, n_head, q_ref, k_ref, v_ref, doc_ref, dq_ref, dk_ref, dv_ref,
    qbuf, kvbuf, dbuf, bias, stage_q, stage_kv, part,
    in_s, in_r, loc_in, doc_s, doc_r, l_s, l_r, g_s, g_r, o_s, o_r, loc_out, rbuf, r_s, r_r,
):
    heads, depth, toks = q_ref.shape
    half = heads // 2
    pieces = half // PIECE
    scale = 1.0 / math.sqrt(depth)
    me = lax.axis_index("ctx") * n_head + lax.axis_index("head")
    chip, core = me // 2, me % 2
    mate = 1 - core
    last = n_ctx * n_head // 2 - 1
    odd = chip % 2
    is_left = (chip == 0) | ((odd == 1) & (chip >= 3) & (chip < last))
    is_right = (chip == 1) | ((odd == 0) & (chip >= 4))
    paired = is_left | is_right
    other_chip = jnp.where(is_left, chip + 1, chip - 1)

    flows = n_ctx - 1
    items = flows * DETOUR
    chained = paired & (chip >= 3)
    flow = (chip + 1) // 4 - 1
    far = (chip + 1) % 4 < 2
    ahead_relay, back_relay = jnp.where(far, last, 1), jnp.where(far, 0, 2)
    relays_ahead = (chip == last) | (chip == 1)
    relays_back = (chip == 0) | (chip == 2)
    relays = relays_ahead | relays_back
    far_relay = (chip == last) | (chip == 0)

    def relay_ends(f):
        left = 4 * f + 4 + jnp.where(far_relay, -1, 1)
        return jnp.where(relays_ahead, left, left + 1), jnp.where(relays_ahead, left + 1, left)

    def device(chip_id, core_id):
        linear = chip_id * 2 + core_id
        return (linear // n_head, linear % n_head)

    mate_id = device(chip, mate)

    def remote(src, dst, send, recv, to):
        return pltpu.make_async_remote_copy(
            src_ref=src, dst_ref=dst, send_sem=send, recv_sem=recv, device_id=to, device_id_type=MESH
        )

    def span(base, p):
        return pl.ds(base + p * PIECE, PIECE)

    def mate_in(i, p):
        src = (q_ref, k_ref, v_ref)[i].at[span(mate * half, p)]
        dst = qbuf.at[core, span(0, p)] if i == 0 else kvbuf.at[i - 1, 2 + core, span(0, p)]
        return remote(src, dst, in_s.at[i, p], in_r.at[i, p], mate_id)

    def own_in(i):
        src = (q_ref, k_ref, v_ref)[i].at[pl.ds(core * half, half)]
        dst = qbuf.at[core] if i == 0 else kvbuf.at[i - 1, 2 + core]
        return pltpu.make_async_copy(src, dst, loc_in.at[i])

    def doc_copy():
        return remote(doc_ref, dbuf.at[core], doc_s.at[0], doc_r.at[0], mate_id)

    def ahead(i, j, p):
        src = (k_ref, v_ref)[i].at[span(j * half, p)]
        return remote(
            src, kvbuf.at[i, core, span(0, p)], l_s.at[i, j, p], l_r.at[i, core, p], device(other_chip, j)
        )

    def ahead_arrival(i, j, p):
        src = (k_ref, v_ref)[i].at[span(j * half, p)]
        return remote(
            src, kvbuf.at[i, j, span(0, p)], l_s.at[i, j, p], l_r.at[i, j, p], device(other_chip, j)
        )

    def back(i, j, p):
        return remote(
            stage_kv.at[i, j, span(0, p)], part.at[i, core, span(0, p)],
            g_s.at[i, j, p], g_r.at[i, core, p], device(other_chip, j),
        )

    def back_arrival(i, j, p):
        return remote(
            stage_kv.at[i, j, span(0, p)], part.at[i, j, span(0, p)],
            g_s.at[i, j, p], g_r.at[i, j, p], device(other_chip, j),
        )

    def ahead_detour(i, j, r):
        p = pieces - DETOUR + r
        src = (k_ref, v_ref)[i].at[span(j * half, p)]
        return remote(
            src, rbuf.at[flow, i, j, r], l_s.at[i, j, p], r_r.at[flow, i, j, r], device(ahead_relay, core)
        )

    def back_detour(i, j, r):
        return remote(
            stage_kv.at[i, j, span(0, r)], rbuf.at[flow, i, j, r],
            g_s.at[i, j, r], r_r.at[flow, i, j, r], device(back_relay, core),
        )

    def detour_arrival(f, i, j, r):
        return remote(
            rbuf.at[f, i, j, r], rbuf.at[f, i, j, r], r_s.at[f, i, j, r], r_r.at[f, i, j, r],
            device(relay_ends(f)[1], j),
        )

    def ahead_onward(f, i, j, r):
        p = pieces - DETOUR + r
        return remote(
            rbuf.at[f, i, j, r], kvbuf.at[i, core, span(0, p)],
            r_s.at[f, i, j, r], l_r.at[i, core, p], device(relay_ends(f)[1], j),
        )

    def back_onward(f, i, j, r):
        return remote(
            rbuf.at[f, i, j, r], part.at[i, core, span(0, r)],
            r_s.at[f, i, j, r], g_r.at[i, core, r], device(relay_ends(f)[1], j),
        )

    def relay(onward, item):
        f, r = item % flows, item // flows
        for j in range(2):
            for i in range(2):
                detour_arrival(f, i, j, r).wait_recv()
                onward(f, i, j, r).start()

    def staged(i, whose, p):
        return stage_q.at[whose, span(0, p)] if i == 0 else stage_kv.at[i - 1, 2 + whose, span(0, p)]

    def mate_out(i, p):
        dst = (dq_ref, dk_ref, dv_ref)[i].at[span(core * half, p)]
        return remote(staged(i, mate, p), dst, o_s.at[i, p], o_r.at[i, p], mate_id)

    def mate_out_arrival(i, p):
        dst = (dq_ref, dk_ref, dv_ref)[i].at[span(mate * half, p)]
        return remote(staged(i, mate, p), dst, o_s.at[i, p], o_r.at[i, p], mate_id)

    def own_out(i, p):
        dst = (dq_ref, dk_ref, dv_ref)[i].at[span(core * half, p)]
        return pltpu.make_async_copy(staged(i, core, p), dst, loc_out.at[i, p])

    def each_step(body):
        lax.fori_loop(0, pieces // STEP, lambda t, carry: (body(t), carry)[1], 0)

    def each(body):
        lax.fori_loop(0, pieces, lambda p, carry: (body(p), carry)[1], 0)

    barrier = pltpu.get_barrier_semaphore()
    pl.semaphore_signal(barrier, inc=1, device_id=mate_id, device_id_type=MESH)

    @pl.when(paired)
    def _():
        for j in range(2):
            pl.semaphore_signal(barrier, inc=1, device_id=device(other_chip, j), device_id_type=MESH)

    @pl.when(chained)
    def _():
        single = jnp.where(is_left, ahead_relay, back_relay)
        double = jnp.where(is_left, back_relay, ahead_relay)
        for to in (device(single, core), device(double, 0), device(double, 1)):
            pl.semaphore_signal(barrier, inc=1, device_id=to, device_id_type=MESH)
        pl.semaphore_wait(barrier, 6)

    @pl.when(relays)
    def _():
        for f in range(flows):
            single, double = relay_ends(f)
            for to in (device(single, core), device(double, 0), device(double, 1)):
                pl.semaphore_signal(barrier, inc=1, device_id=to, device_id_type=MESH)

    @pl.when(relays & paired)
    def _():
        pl.semaphore_wait(barrier, 3 + 3 * flows)

    @pl.when(relays & jnp.logical_not(paired))
    def _():
        pl.semaphore_wait(barrier, 1 + 3 * flows)

    @pl.when(is_left)
    def _():
        def send(p):
            for j in range(2):
                for i in range(2):
                    ahead(i, j, p).start()

        @pl.when(chained)
        def _():
            for r in range(DETOUR):
                for j in range(2):
                    for i in range(2):
                        ahead_detour(i, j, r).start()

        lax.fori_loop(0, pieces - DETOUR, lambda p, carry: (send(p), carry)[1], 0)

        @pl.when(jnp.logical_not(chained))
        def _():
            for r in range(DETOUR):
                send(pieces - DETOUR + r)

    doc_copy().start()
    for i in range(3):
        own_in(i).start()

    def send_mate(p):
        for i in range(3):
            mate_in(i, p).start()

    each(send_mate)
    dbuf[core] = doc_ref[...]
    for i in range(3):
        own_in(i).wait()
    doc_copy().wait_send()
    remote(doc_ref, dbuf.at[mate], doc_s.at[0], doc_r.at[0], mate_id).wait_recv()

    wide = 2 * toks
    base = chip * wide
    first = jnp.concatenate([dbuf[0], dbuf[1]], axis=1)
    query_pos = base + lax.broadcasted_iota(jnp.int32, (2 * wide, wide), 1)
    key_pos = base - wide + lax.broadcasted_iota(jnp.int32, (2 * wide, wide), 0)
    bias[...] = jnp.where((key_pos >= first) & (key_pos <= query_pos), 0.0, -jnp.inf)

    def some_heads(first_head, slots):
        hs = [first_head + n for n in range(STEP * PIECE)]
        rows = pl.ds(slots[0] * toks, len(slots) * toks)
        dot = functools.partial(lax.dot_general, preferred_element_type=jnp.float32)
        tn, nn, nt = ((((0,), (0,)), ((), ())), (((1,), (0,)), ((), ())), (((1,), (1,)), ((), ())))

        def query(h):
            return jnp.concatenate([qbuf[0, h], qbuf[1, h]], axis=1)

        def window(i, h):
            return jnp.concatenate([kvbuf[i, s, h] for s in slots], axis=1)

        scores = [dot(window(0, h), query(h), tn) for h in hs]
        probs, low, attended, grad_scores = [], [], [], []
        for h, raw in zip(hs, scores):
            raw = raw * (scale * math.log2(math.e)) + bias[rows, :]
            weights = jnp.exp2(raw - jnp.max(raw, axis=0, keepdims=True))
            probs.append(weights * (1.0 / jnp.sum(weights, axis=0, keepdims=True)))
            low.append(probs[-1].astype(jnp.bfloat16))
            attended.append(dot(window(1, h), low[-1], nn).astype(jnp.bfloat16))
        grad_probs = [dot(window(1, h), att, tn) for h, att in zip(hs, attended)]
        for n, h in enumerate(hs):
            wide_att = attended[n].astype(jnp.float32)
            row_dot = jnp.sum(wide_att * wide_att, axis=0, keepdims=True)
            grad_scores.append((probs[n] * (grad_probs[n] - row_dot)).astype(jnp.bfloat16))
            grad_v = dot(attended[n], low[n], nt).astype(jnp.bfloat16)
            for m, s in enumerate(slots):
                stage_kv[1, s, h] = grad_v[:, m * toks : (m + 1) * toks]
        for n, h in enumerate(hs):
            grad_q = (dot(window(0, h), grad_scores[n], nn) * scale).astype(jnp.bfloat16)
            grad_k = (dot(query(h), grad_scores[n], nt) * scale).astype(jnp.bfloat16)
            for j in range(2):
                stage_q[j, h] = grad_q[:, j * toks : (j + 1) * toks]
            for m, s in enumerate(slots):
                stage_kv[0, s, h] = grad_k[:, m * toks : (m + 1) * toks]

    def work(t, slots):
        for n in range(STEP):
            p = t * STEP + n
            for i in range(3):
                dst = qbuf.at[mate, span(0, p)] if i == 0 else kvbuf.at[i - 1, 2 + mate, span(0, p)]
                src = (q_ref, k_ref, v_ref)[i].at[span(mate * half, p)]
                remote(src, dst, in_s.at[i, p], in_r.at[i, p], mate_id).wait_recv()
        some_heads(t * STEP * PIECE, slots)
        for n in range(STEP):
            for i in range(3):
                mate_out(i, t * STEP + n).start()
                own_out(i, t * STEP + n).start()

    def relay_step(t):
        for n in range(STEP):
            @pl.when(t * STEP + n < items)
            def _():
                relay(ahead_onward, t * STEP + n)

    @pl.when(is_right)
    def _():
        def send_back(p):
            for j in range(2):
                for i in range(2):
                    back(i, j, p).start()

        def send_detour(r):
            for j in range(2):
                for i in range(2):
                    back_detour(i, j, r).start()

        def send_most():
            @pl.when(jnp.logical_not(far))
            def _():
                for r in range(DETOUR):
                    send_detour(r)

            lax.fori_loop(DETOUR, pieces - 2 * STEP, lambda e, carry: (send_back(e), carry)[1], 0)

        def step(t):
            for n in range(STEP):
                for j in range(2):
                    for i in range(2):
                        ahead_arrival(i, j, t * STEP + n).wait_recv()

            @pl.when(chained & (t == pieces // STEP - 2))
            def _():
                send_most()

            work(t, (0, 1, 2, 3))

            for n in range(STEP):
                @pl.when(chained & far & (t * STEP + n < DETOUR))
                def _():
                    send_detour(t * STEP + n)

            @pl.when(jnp.logical_not(chained) | (t >= pieces // STEP - 2))
            def _():
                for n in range(STEP):
                    send_back(t * STEP + n)

            @pl.when(jnp.logical_not(chained))
            def _():
                relay_step(t)

        each_step(step)

    @pl.when(jnp.logical_not(is_right))
    def _():
        def step(t):
            work(t, (2, 3))

            @pl.when(chip == last)
            def _():
                relay_step(t)

        each_step(step)

    def drain(p):
        for i in range(3):
            mate_in(i, p).wait_send()
            own_out(i, p).wait()
            mate_out(i, p).wait_send()
            mate_out_arrival(i, p).wait_recv()

    each(drain)

    @pl.when(relays_back)
    def _():
        lax.fori_loop(0, items, lambda t, carry: (relay(back_onward, t), carry)[1], 0)

    @pl.when(is_left)
    def _():
        def add(p):
            for i in range(2):
                out = (dk_ref, dv_ref)[i]
                for j in range(2):
                    ahead(i, j, p).wait_send()
                    back_arrival(i, j, p).wait_recv()
                    at = span(j * half, p)
                    total = out[at].astype(jnp.float32) + part[i, j, span(0, p)].astype(jnp.float32)
                    out[at] = total.astype(jnp.bfloat16)

        each(add)

    @pl.when(is_right)
    def _():
        def sent(p):
            for j in range(2):
                for i in range(2):
                    back(i, j, p).wait_send()

        each(sent)

    @pl.when(relays)
    def _():
        def onward_sent(t):
            for j in range(2):
                for i in range(2):
                    ahead_onward(t % flows, i, j, t // flows).wait_send()

        lax.fori_loop(0, items, lambda t, carry: (onward_sent(t), carry)[1], 0)


def chunk_shards(n_ctx, n_head, queries, keys, values, doc_start):
    heads, depth, toks = queries.shape
    half = heads // 2
    pieces = half // PIECE
    like = jax.ShapeDtypeStruct(queries.shape, jnp.bfloat16)
    vmem = pl.BlockSpec(memory_space=pltpu.VMEM)
    low, sem = jnp.bfloat16, pltpu.SemaphoreType.DMA
    return pl.pallas_call(
        functools.partial(chunk_kernel, n_ctx, n_head),
        out_shape=(like, like, like),
        in_specs=[pl.BlockSpec(memory_space=pltpu.HBM)] * 3 + [vmem],
        out_specs=(vmem,) * 3,
        scratch_shapes=[
            pltpu.VMEM((2, half, depth, toks), low),
            pltpu.VMEM((2, 4, half, depth, toks), low),
            pltpu.VMEM((2, 1, toks), jnp.int32),
            pltpu.VMEM((4 * toks, 2 * toks), jnp.float32),
            pltpu.VMEM((2, half, depth, toks), low),
            pltpu.VMEM((2, 4, half, depth, toks), low),
            pltpu.VMEM((2, 2, half, depth, toks), low),
            sem((3, pieces)), sem((3, pieces)), sem((3,)), sem((1,)), sem((1,)),
            sem((2, 2, pieces)), sem((2, 2, pieces)), sem((2, 2, pieces)), sem((2, 2, pieces)),
            sem((3, pieces)), sem((3, pieces)), sem((3, pieces)),
            pltpu.VMEM((n_ctx - 1, 2, 2, DETOUR, PIECE, depth, toks), low),
            sem((n_ctx - 1, 2, 2, DETOUR)), sem((n_ctx - 1, 2, 2, DETOUR)),
        ],
        compiler_params=pltpu.CompilerParams(
            collective_id=0, has_side_effects=True, vmem_limit_bytes=60 * 1024 * 1024
        ),
        cost_estimate=pl.CostEstimate(
            flops=12 * half * 8 * toks * toks * depth, bytes_accessed=12 * heads * depth * toks,
            transcendentals=8 * half * toks * toks,
        ),
    )(queries, keys, values, doc_start.reshape(1, toks))


def solution(mesh):
    n_ctx, n_head = mesh.shape["ctx"], mesh.shape["head"]

    def program(queries, keys, values, doc_start):
        toks = queries.shape[2]
        pieces = queries.shape[0] // (2 * PIECE)
        fits = queries.shape[0] % (2 * PIECE * STEP) == 0 and 1 < n_ctx and (n_ctx - 1) * DETOUR <= pieces - 2 * STEP
        if 4 * toks == DOC_MAX and n_head * toks == 2 * DOC_MAX and fits:
            return chunk_shards(n_ctx, n_head, queries, keys, values, doc_start)
        return shards(queries, keys, values, doc_start)

    spec = P(None, None, ("ctx", "head"))
    return jax.shard_map(
        program,
        mesh=mesh,
        in_specs=(spec, spec, spec, P(("ctx", "head"))),
        out_specs=(spec, spec, spec),
        check_vma=False,
    )
```

```python
import functools
import math

import jax
import jax.numpy as jnp
from jax import lax
from jax.experimental import pallas as pl
from jax.experimental.pallas import tpu as pltpu
from jax.sharding import PartitionSpec as P

DOC_MAX = 512
PIECE = 1
STEP = 2
DETOUR = 3
MESH = pl.DeviceIdType.MESH


def from_behind(value, axis, steps):
    count = lax.axis_size(axis)
    first, last = (max(0, -steps), min(count, count - steps))
    return lax.ppermute(value, axis, [(source, source + steps) for source in range(first, last)])


def block_grads(query_blk, key_win, value_win, first_pos, query_pos, key_pos, score_scale):
    visible = (key_pos[None, :] >= first_pos[:, None]) & (key_pos[None, :] <= query_pos[:, None])
    scores = (
        jnp.einsum("hdq,hdk->hqk", query_blk, key_win, preferred_element_type=jnp.float32)
        * score_scale
    )
    scores = jnp.where(visible[None], scores, -jnp.inf)
    row_peak = jnp.max(scores, axis=2, keepdims=True)
    weights = jnp.exp(scores - row_peak)
    soft_probs = weights / jnp.sum(weights, axis=2, keepdims=True)
    probs_low = soft_probs.astype(jnp.bfloat16)
    attended = jnp.einsum(
        "hqk,hdk->hdq", probs_low, value_win, preferred_element_type=jnp.float32
    ).astype(jnp.bfloat16)
    grad_value = jnp.einsum("hqk,hdq->hdk", probs_low, attended, preferred_element_type=jnp.float32)
    grad_probs = jnp.einsum("hdq,hdk->hqk", attended, value_win, preferred_element_type=jnp.float32)
    wide_att = attended.astype(jnp.float32)
    row_dot = jnp.sum(wide_att * wide_att, axis=1)
    grad_scores = (soft_probs * (grad_probs - row_dot[:, :, None])).astype(jnp.bfloat16)
    grad_query = (
        jnp.einsum("hqk,hdk->hdq", grad_scores, key_win, preferred_element_type=jnp.float32)
        * score_scale
    ).astype(jnp.bfloat16)
    grad_key = jnp.einsum(
        "hqk,hdq->hdk", grad_scores, query_blk, preferred_element_type=jnp.float32
    )
    return (grad_query, grad_key, grad_value)


def shards(queries, keys, values, doc_start):
    score_scale = 1.0 / math.sqrt(queries.shape[1])
    head_q, head_k, head_v = (
        lax.all_to_all(queries, "head", split_axis=0, concat_axis=2, tiled=True),
        lax.all_to_all(keys, "head", split_axis=0, concat_axis=2, tiled=True),
        lax.all_to_all(values, "head", split_axis=0, concat_axis=2, tiled=True),
    )
    starts = lax.all_gather(doc_start, "head", axis=0, tiled=True)
    local_heads = head_q.shape[0]
    head_depth = head_q.shape[1]
    group_span = head_q.shape[2]
    window = DOC_MAX
    blocks = group_span // window
    prior_k, prior_v = from_behind(
        (head_k[:, :, group_span - window :], head_v[:, :, group_span - window :]), "ctx", 1
    )
    anchor = lax.axis_index("ctx") * group_span
    key_ext = jnp.concatenate([prior_k, head_k], axis=2).reshape(
        local_heads, head_depth, blocks + 1, window
    )
    value_ext = jnp.concatenate([prior_v, head_v], axis=2).reshape(
        local_heads, head_depth, blocks + 1, window
    )
    key_wins = jnp.moveaxis(jnp.concatenate([key_ext[:, :, :-1], key_ext[:, :, 1:]], axis=3), 2, 0)
    value_wins = jnp.moveaxis(
        jnp.concatenate([value_ext[:, :, :-1], value_ext[:, :, 1:]], axis=3), 2, 0
    )
    query_blocks = jnp.moveaxis(head_q.reshape(local_heads, head_depth, blocks, window), 2, 0)
    start_blocks = starts.reshape(blocks, window)
    offsets = jnp.arange(window, dtype=jnp.int32)
    spread = jnp.arange(2 * window, dtype=jnp.int32)

    def one_block(unused_carry, block_item):
        query_blk, key_win, value_win, first_pos, number = block_item
        block_base = anchor + number * window
        query_pos = block_base + offsets
        key_pos = block_base - window + spread
        return (
            unused_carry,
            block_grads(query_blk, key_win, value_win, first_pos, query_pos, key_pos, score_scale),
        )

    _, (query_stack, key_stack, value_stack) = lax.scan(
        one_block,
        jnp.int32(0),
        (query_blocks, key_wins, value_wins, start_blocks, jnp.arange(blocks, dtype=jnp.int32)),
    )
    far_k = key_stack[..., :window]
    far_v = value_stack[..., :window]
    own_k = key_stack[..., window:] + jnp.concatenate(
        [far_k[1:], jnp.zeros_like(far_k[:1])], axis=0
    )
    own_v = value_stack[..., window:] + jnp.concatenate(
        [far_v[1:], jnp.zeros_like(far_v[:1])], axis=0
    )
    back_k, back_v = from_behind((far_k[0], far_v[0]), "ctx", -1)
    own_k = own_k.at[blocks - 1].add(back_k)
    own_v = own_v.at[blocks - 1].add(back_v)

    def to_span(stacked):
        return jnp.moveaxis(stacked, 0, 2).reshape(local_heads, head_depth, group_span)

    grad_q = to_span(query_stack)
    grad_k = (to_span(own_k) * score_scale).astype(jnp.bfloat16)
    grad_v = to_span(own_v).astype(jnp.bfloat16)
    return (
        lax.all_to_all(grad_q, "head", split_axis=2, concat_axis=0, tiled=True),
        lax.all_to_all(grad_k, "head", split_axis=2, concat_axis=0, tiled=True),
        lax.all_to_all(grad_v, "head", split_axis=2, concat_axis=0, tiled=True),
    )


def chunk_kernel(
    n_ctx, n_head, q_ref, k_ref, v_ref, doc_ref, dq_ref, dk_ref, dv_ref,
    qbuf, kvbuf, dbuf, bias, stage_q, stage_kv, part,
    in_s, in_r, loc_in, doc_s, doc_r, l_s, l_r, g_s, g_r, o_s, o_r, loc_out, rbuf, r_s, r_r,
):
    heads, depth, toks = q_ref.shape
    half = heads // 2
    pieces = half // PIECE
    scale = 1.0 / math.sqrt(depth)
    me = lax.axis_index("ctx") * n_head + lax.axis_index("head")
    chip, core = me // 2, me % 2
    mate = 1 - core
    last = n_ctx * n_head // 2 - 1
    odd = chip % 2
    is_left = (chip == 0) | ((odd == 1) & (chip >= 3) & (chip < last))
    is_right = (chip == 1) | ((odd == 0) & (chip >= 4))
    paired = is_left | is_right
    other_chip = jnp.where(is_left, chip + 1, chip - 1)

    flows = n_ctx - 1
    items = flows * DETOUR
    chained = paired & (chip >= 3)
    flow = (chip + 1) // 4 - 1
    far = (chip + 1) % 4 < 2
    ahead_relay, back_relay = jnp.where(far, last, 1), jnp.where(far, 0, 2)
    relays_ahead = (chip == last) | (chip == 1)
    relays_back = (chip == 0) | (chip == 2)
    relays = relays_ahead | relays_back
    far_relay = (chip == last) | (chip == 0)

    def relay_ends(f):
        left = 4 * f + 4 + jnp.where(far_relay, -1, 1)
        return jnp.where(relays_ahead, left, left + 1), jnp.where(relays_ahead, left + 1, left)

    def device(chip_id, core_id):
        linear = chip_id * 2 + core_id
        return (linear // n_head, linear % n_head)

    mate_id = device(chip, mate)

    def remote(src, dst, send, recv, to):
        return pltpu.make_async_remote_copy(
            src_ref=src, dst_ref=dst, send_sem=send, recv_sem=recv, device_id=to, device_id_type=MESH
        )

    def span(base, p):
        return pl.ds(base + p * PIECE, PIECE)

    def mate_in(i, p):
        src = (q_ref, k_ref, v_ref)[i].at[span(mate * half, p)]
        dst = qbuf.at[core, span(0, p)] if i == 0 else kvbuf.at[i - 1, 2 + core, span(0, p)]
        return remote(src, dst, in_s.at[i, p], in_r.at[i, p], mate_id)

    def own_in(i):
        src = (q_ref, k_ref, v_ref)[i].at[pl.ds(core * half, half)]
        dst = qbuf.at[core] if i == 0 else kvbuf.at[i - 1, 2 + core]
        return pltpu.make_async_copy(src, dst, loc_in.at[i])

    def doc_copy():
        return remote(doc_ref, dbuf.at[core], doc_s.at[0], doc_r.at[0], mate_id)

    def ahead(i, j, p):
        src = (k_ref, v_ref)[i].at[span(j * half, p)]
        return remote(
            src, kvbuf.at[i, core, span(0, p)], l_s.at[i, j, p], l_r.at[i, core, p], device(other_chip, j)
        )

    def ahead_arrival(i, j, p):
        src = (k_ref, v_ref)[i].at[span(j * half, p)]
        return remote(
            src, kvbuf.at[i, j, span(0, p)], l_s.at[i, j, p], l_r.at[i, j, p], device(other_chip, j)
        )

    def back(i, j, p):
        return remote(
            stage_kv.at[i, j, span(0, p)], part.at[i, core, span(0, p)],
            g_s.at[i, j, p], g_r.at[i, core, p], device(other_chip, j),
        )

    def back_arrival(i, j, p):
        return remote(
            stage_kv.at[i, j, span(0, p)], part.at[i, j, span(0, p)],
            g_s.at[i, j, p], g_r.at[i, j, p], device(other_chip, j),
        )

    def ahead_detour(i, j, r):
        p = pieces - DETOUR + r
        src = (k_ref, v_ref)[i].at[span(j * half, p)]
        return remote(
            src, rbuf.at[flow, i, j, r], l_s.at[i, j, p], r_r.at[flow, i, j, r], device(ahead_relay, core)
        )

    def back_detour(i, j, r):
        return remote(
            stage_kv.at[i, j, span(0, r)], rbuf.at[flow, i, j, r],
            g_s.at[i, j, r], r_r.at[flow, i, j, r], device(back_relay, core),
        )

    def detour_arrival(f, i, j, r):
        return remote(
            rbuf.at[f, i, j, r], rbuf.at[f, i, j, r], r_s.at[f, i, j, r], r_r.at[f, i, j, r],
            device(relay_ends(f)[1], j),
        )

    def ahead_onward(f, i, j, r):
        p = pieces - DETOUR + r
        return remote(
            rbuf.at[f, i, j, r], kvbuf.at[i, core, span(0, p)],
            r_s.at[f, i, j, r], l_r.at[i, core, p], device(relay_ends(f)[1], j),
        )

    def back_onward(f, i, j, r):
        return remote(
            rbuf.at[f, i, j, r], part.at[i, core, span(0, r)],
            r_s.at[f, i, j, r], g_r.at[i, core, r], device(relay_ends(f)[1], j),
        )

    def relay(onward, item):
        f, r = item % flows, item // flows
        for j in range(2):
            for i in range(2):
                detour_arrival(f, i, j, r).wait_recv()
                onward(f, i, j, r).start()

    def staged(i, whose, p):
        return stage_q.at[whose, span(0, p)] if i == 0 else stage_kv.at[i - 1, 2 + whose, span(0, p)]

    def mate_out(i, p):
        dst = (dq_ref, dk_ref, dv_ref)[i].at[span(core * half, p)]
        return remote(staged(i, mate, p), dst, o_s.at[i, p], o_r.at[i, p], mate_id)

    def mate_out_arrival(i, p):
        dst = (dq_ref, dk_ref, dv_ref)[i].at[span(mate * half, p)]
        return remote(staged(i, mate, p), dst, o_s.at[i, p], o_r.at[i, p], mate_id)

    def own_out(i, p):
        dst = (dq_ref, dk_ref, dv_ref)[i].at[span(core * half, p)]
        return pltpu.make_async_copy(staged(i, core, p), dst, loc_out.at[i, p])

    def each_step(body):
        lax.fori_loop(0, pieces // STEP, lambda t, carry: (body(t), carry)[1], 0)

    def each(body):
        lax.fori_loop(0, pieces, lambda p, carry: (body(p), carry)[1], 0)

    barrier = pltpu.get_barrier_semaphore()
    pl.semaphore_signal(barrier, inc=1, device_id=mate_id, device_id_type=MESH)

    @pl.when(paired)
    def _():
        for j in range(2):
            pl.semaphore_signal(barrier, inc=1, device_id=device(other_chip, j), device_id_type=MESH)

    @pl.when(chained)
    def _():
        single = jnp.where(is_left, ahead_relay, back_relay)
        double = jnp.where(is_left, back_relay, ahead_relay)
        for to in (device(single, core), device(double, 0), device(double, 1)):
            pl.semaphore_signal(barrier, inc=1, device_id=to, device_id_type=MESH)
        pl.semaphore_wait(barrier, 6)

    @pl.when(relays)
    def _():
        for f in range(flows):
            single, double = relay_ends(f)
            for to in (device(single, core), device(double, 0), device(double, 1)):
                pl.semaphore_signal(barrier, inc=1, device_id=to, device_id_type=MESH)

    @pl.when(relays & paired)
    def _():
        pl.semaphore_wait(barrier, 3 + 3 * flows)

    @pl.when(relays & jnp.logical_not(paired))
    def _():
        pl.semaphore_wait(barrier, 1 + 3 * flows)

    @pl.when(is_left)
    def _():
        def send(p):
            for j in range(2):
                for i in range(2):
                    ahead(i, j, p).start()

        @pl.when(chained)
        def _():
            for r in range(DETOUR):
                for j in range(2):
                    for i in range(2):
                        ahead_detour(i, j, r).start()

        lax.fori_loop(0, pieces - DETOUR, lambda p, carry: (send(p), carry)[1], 0)

        @pl.when(jnp.logical_not(chained))
        def _():
            for r in range(DETOUR):
                send(pieces - DETOUR + r)

    doc_copy().start()
    for i in range(3):
        own_in(i).start()

    def send_mate(p):
        for i in range(3):
            mate_in(i, p).start()

    each(send_mate)
    dbuf[core] = doc_ref[...]
    for i in range(3):
        own_in(i).wait()
    doc_copy().wait_send()
    remote(doc_ref, dbuf.at[mate], doc_s.at[0], doc_r.at[0], mate_id).wait_recv()

    wide = 2 * toks
    base = chip * wide
    first = jnp.concatenate([dbuf[0], dbuf[1]], axis=1)
    query_pos = base + lax.broadcasted_iota(jnp.int32, (2 * wide, wide), 1)
    key_pos = base - wide + lax.broadcasted_iota(jnp.int32, (2 * wide, wide), 0)
    bias[...] = jnp.where((key_pos >= first) & (key_pos <= query_pos), 0.0, -jnp.inf)

    def some_heads(first_head, slots):
        hs = [first_head + n for n in range(STEP * PIECE)]
        rows = pl.ds(slots[0] * toks, len(slots) * toks)
        dot = functools.partial(lax.dot_general, preferred_element_type=jnp.float32)
        tn, nn, nt = ((((0,), (0,)), ((), ())), (((1,), (0,)), ((), ())), (((1,), (1,)), ((), ())))

        def query(h):
            return jnp.concatenate([qbuf[0, h], qbuf[1, h]], axis=1)

        def window(i, h):
            return jnp.concatenate([kvbuf[i, s, h] for s in slots], axis=1)

        scores = [dot(window(0, h), query(h), tn) for h in hs]
        probs, low, attended, grad_scores = [], [], [], []
        for h, raw in zip(hs, scores):
            raw = raw * (scale * math.log2(math.e)) + bias[rows, :]
            weights = jnp.exp2(raw - jnp.max(raw, axis=0, keepdims=True))
            probs.append(weights * (1.0 / jnp.sum(weights, axis=0, keepdims=True)))
            low.append(probs[-1].astype(jnp.bfloat16))
            attended.append(dot(window(1, h), low[-1], nn).astype(jnp.bfloat16))
        grad_probs = [dot(window(1, h), att, tn) for h, att in zip(hs, attended)]
        for n, h in enumerate(hs):
            wide_att = attended[n].astype(jnp.float32)
            row_dot = jnp.sum(wide_att * wide_att, axis=0, keepdims=True)
            grad_scores.append((probs[n] * (grad_probs[n] - row_dot)).astype(jnp.bfloat16))
            grad_v = dot(attended[n], low[n], nt).astype(jnp.bfloat16)
            for m, s in enumerate(slots):
                stage_kv[1, s, h] = grad_v[:, m * toks : (m + 1) * toks]
        for n, h in enumerate(hs):
            grad_q = (dot(window(0, h), grad_scores[n], nn) * scale).astype(jnp.bfloat16)
            grad_k = (dot(query(h), grad_scores[n], nt) * scale).astype(jnp.bfloat16)
            for j in range(2):
                stage_q[j, h] = grad_q[:, j * toks : (j + 1) * toks]
            for m, s in enumerate(slots):
                stage_kv[0, s, h] = grad_k[:, m * toks : (m + 1) * toks]

    def work(t, slots):
        for n in range(STEP):
            p = t * STEP + n
            for i in range(3):
                dst = qbuf.at[mate, span(0, p)] if i == 0 else kvbuf.at[i - 1, 2 + mate, span(0, p)]
                src = (q_ref, k_ref, v_ref)[i].at[span(mate * half, p)]
                remote(src, dst, in_s.at[i, p], in_r.at[i, p], mate_id).wait_recv()
        some_heads(t * STEP * PIECE, slots)
        for n in range(STEP):
            for i in range(3):
                mate_out(i, t * STEP + n).start()
                own_out(i, t * STEP + n).start()

    def relay_step(t):
        for n in range(STEP):
            @pl.when(t * STEP + n < items)
            def _():
                relay(ahead_onward, t * STEP + n)

    @pl.when(is_right)
    def _():
        def send_back(p):
            for j in range(2):
                for i in range(2):
                    back(i, j, p).start()

        def send_detour(r):
            for j in range(2):
                for i in range(2):
                    back_detour(i, j, r).start()

        def send_most():
            @pl.when(jnp.logical_not(far))
            def _():
                for r in range(DETOUR):
                    send_detour(r)

            lax.fori_loop(DETOUR, pieces - 2 * STEP, lambda e, carry: (send_back(e), carry)[1], 0)

        def step(t):
            for n in range(STEP):
                for j in range(2):
                    for i in range(2):
                        ahead_arrival(i, j, t * STEP + n).wait_recv()

            @pl.when(chained & (t == pieces // STEP - 2))
            def _():
                send_most()

            work(t, (0, 1, 2, 3))

            for n in range(STEP):
                @pl.when(chained & far & (t * STEP + n < DETOUR))
                def _():
                    send_detour(t * STEP + n)

            @pl.when(jnp.logical_not(chained) | (t >= pieces // STEP - 2))
            def _():
                for n in range(STEP):
                    send_back(t * STEP + n)

            @pl.when(jnp.logical_not(chained))
            def _():
                relay_step(t)

        each_step(step)

    @pl.when(jnp.logical_not(is_right))
    def _():
        def step(t):
            work(t, (2, 3))

            @pl.when(chip == last)
            def _():
                relay_step(t)

        each_step(step)

    def drain(p):
        for i in range(3):
            mate_in(i, p).wait_send()
            own_out(i, p).wait()
            mate_out(i, p).wait_send()
            mate_out_arrival(i, p).wait_recv()

    each(drain)

    def ahead_sent(p):
        for j in range(2):
            for i in range(2):
                ahead(i, j, p).wait_send()

    @pl.when(is_left & relays_back)
    def _():
        each(ahead_sent)

    @pl.when(relays_back)
    def _():
        lax.fori_loop(0, items, lambda t, carry: (relay(back_onward, t), carry)[1], 0)

    @pl.when(is_left & jnp.logical_not(relays_back))
    def _():
        each(ahead_sent)

    @pl.when(is_left)
    def _():
        def add(p):
            for i in range(2):
                out = (dk_ref, dv_ref)[i]
                for j in range(2):
                    back_arrival(i, j, p).wait_recv()
                    at = span(j * half, p)
                    total = out[at].astype(jnp.float32) + part[i, j, span(0, p)].astype(jnp.float32)
                    out[at] = total.astype(jnp.bfloat16)

        each(add)

    @pl.when(is_right)
    def _():
        def sent(p):
            for j in range(2):
                for i in range(2):
                    back(i, j, p).wait_send()

        each(sent)

    @pl.when(relays)
    def _():
        def onward_sent(t):
            for j in range(2):
                for i in range(2):
                    ahead_onward(t % flows, i, j, t // flows).wait_send()

        lax.fori_loop(0, items, lambda t, carry: (onward_sent(t), carry)[1], 0)


def chunk_shards(n_ctx, n_head, queries, keys, values, doc_start):
    heads, depth, toks = queries.shape
    half = heads // 2
    pieces = half // PIECE
    like = jax.ShapeDtypeStruct(queries.shape, jnp.bfloat16)
    vmem = pl.BlockSpec(memory_space=pltpu.VMEM)
    low, sem = jnp.bfloat16, pltpu.SemaphoreType.DMA
    return pl.pallas_call(
        functools.partial(chunk_kernel, n_ctx, n_head),
        out_shape=(like, like, like),
        in_specs=[pl.BlockSpec(memory_space=pltpu.HBM)] * 3 + [vmem],
        out_specs=(vmem,) * 3,
        scratch_shapes=[
            pltpu.VMEM((2, half, depth, toks), low),
            pltpu.VMEM((2, 4, half, depth, toks), low),
            pltpu.VMEM((2, 1, toks), jnp.int32),
            pltpu.VMEM((4 * toks, 2 * toks), jnp.float32),
            pltpu.VMEM((2, half, depth, toks), low),
            pltpu.VMEM((2, 4, half, depth, toks), low),
            pltpu.VMEM((2, 2, half, depth, toks), low),
            sem((3, pieces)), sem((3, pieces)), sem((3,)), sem((1,)), sem((1,)),
            sem((2, 2, pieces)), sem((2, 2, pieces)), sem((2, 2, pieces)), sem((2, 2, pieces)),
            sem((3, pieces)), sem((3, pieces)), sem((3, pieces)),
            pltpu.VMEM((n_ctx - 1, 2, 2, DETOUR, PIECE, depth, toks), low),
            sem((n_ctx - 1, 2, 2, DETOUR)), sem((n_ctx - 1, 2, 2, DETOUR)),
        ],
        compiler_params=pltpu.CompilerParams(
            collective_id=0, has_side_effects=True, vmem_limit_bytes=60 * 1024 * 1024
        ),
        cost_estimate=pl.CostEstimate(
            flops=12 * half * 8 * toks * toks * depth, bytes_accessed=12 * heads * depth * toks,
            transcendentals=8 * half * toks * toks,
        ),
    )(queries, keys, values, doc_start.reshape(1, toks))


def solution(mesh):
    n_ctx, n_head = mesh.shape["ctx"], mesh.shape["head"]

    def program(queries, keys, values, doc_start):
        toks = queries.shape[2]
        pieces = queries.shape[0] // (2 * PIECE)
        fits = queries.shape[0] % (2 * PIECE * STEP) == 0 and 1 < n_ctx and (n_ctx - 1) * DETOUR <= pieces - 2 * STEP
        if 4 * toks == DOC_MAX and n_head * toks == 2 * DOC_MAX and fits:
            return chunk_shards(n_ctx, n_head, queries, keys, values, doc_start)
        return shards(queries, keys, values, doc_start)

    spec = P(None, None, ("ctx", "head"))
    return jax.shard_map(
        program,
        mesh=mesh,
        in_specs=(spec, spec, spec, P(("ctx", "head"))),
        out_specs=(spec, spec, spec),
        check_vma=False,
    )
```
